512 devices in a mesh: dp: 64 (over x, z), tensor: 8 (over y, core).
Axes of the slice: x: 4, y: 4, z: 16, core: 2. Of those that a mesh axis runs over, the one named last changes fastest.
Arguments:
- inputs: bfloat16 [16384, 1024], P('dp'), may hold values from -6 to 6
- out_grad: bfloat16 [16384, 8192], P('dp', 'tensor')
- left_stat: float32 [64, 512, 512], P('dp', 'tensor')
- right_stat: float32 [64, 512, 512], P('dp', 'tensor')
- left_root: float32 [64, 512, 512], P('dp', 'tensor')
- right_root: float32 [64, 512, 512], P('dp', 'tensor'), as said below
- owner_blocks: int32 [64, 1], replicated, may hold values from 0 to 32, as said below
Outputs:
- left_new: float32 [64, 512, 512], P('dp', 'tensor')
- right_new: float32 [64, 512, 512], P('dp', 'tensor')
- direction: bfloat16 [1024, 8192], P('dp', 'tensor')
The draws below stay inside these ranges and needn't reach their ends.
Inputs may be any that keep to these rules, and one draw needn't show every extreme that they name: `owner_blocks`: each of the 32 blocks appears in exactly one slot; every other slot holds 32; some owners hold a block while others hold none. `right_root`: each slot's matrix is symmetric.
All inputs are finite; a program needn't handle non-finite values.
Results may differ from the reference program's by a relative error of at most 0.00115.
Values may be sent and summed in bfloat16 or wider, within the bound.
A program may use at most 64 MiB of HBM per device.

```python
import jax
import jax.numpy as jnp
from jax import lax

BLK = 512
RB = 2
CBD = 2
CAP = 1
NB = 32
SLOTS = 64
WR = 1024
WC = 8192
TOKENS = 16384
N_DP = 64
N_TENSOR = 8


def symmetric_draw(key, low_diag, high_diag, spread):
    key_normal = jax.random.fold_in(key, 0)
    key_diag = jax.random.fold_in(key, 2)
    shape = (N_DP * CAP, BLK, BLK)
    noise = jax.random.normal(key_normal, shape, jnp.float32)
    paired = (noise + jnp.swapaxes(noise, 1, 2)) * 0.70710678
    diagonal = jax.random.uniform(key_diag, (N_DP * CAP, BLK), jnp.float32, low_diag, high_diag)
    identity = jnp.eye(BLK, dtype=jnp.float32)
    return paired * (spread * BLK ** (-0.5)) * (1.0 - identity) + identity * diagonal[:, :, None]


def draw_left_stat(key, part):
    key = jax.random.fold_in(key, 3)
    return symmetric_draw(key, 0.5, 1.5, 0.25)


def draw_right_stat(key, part):
    key = jax.random.fold_in(key, 5)
    return symmetric_draw(key, 0.5, 1.5, 0.25)


def draw_left_root(key, part):
    key = jax.random.fold_in(key, 9)
    return symmetric_draw(key, 0.6, 1.4, 0.25)


def draw_right_root(key, part):
    key = jax.random.fold_in(key, 13)
    return symmetric_draw(key, 0.6, 1.4, 0.25)


def draw_out_grad(key, part):
    key = jax.random.fold_in(key, 7)
    key_entries, key_jitter = jax.random.split(key, 2)
    column = (jnp.arange(WC) % BLK).astype(jnp.float32)
    column_rise = 1.0 + 2.0 * column / BLK
    jitter = jnp.exp(jax.random.uniform(key_jitter, (WC,), jnp.float32, -0.35, 0.35))
    entries = jax.random.normal(key_entries, (TOKENS, WC), jnp.float32)
    return (entries * column_rise * jitter * TOKENS ** (-0.5)).astype(jnp.bfloat16)


def draw_owner_blocks(key, part):
    key = jax.random.fold_in(key, 11)
    key_order, key_hosts = jax.random.split(key)
    total = RB * CBD * N_TENSOR
    order = jax.random.permutation(key_order, total).astype(jnp.int32)
    hosts = jax.random.permutation(key_hosts, N_DP).astype(jnp.int32)
    table = jnp.full((N_DP, CAP), total, jnp.int32)
    table = table.at[hosts[:total], 0].set(order)
    return table


def steps_of(own_key, shape, cuts, least, top_value):
    loudness, own = 1.0, jax.random.fold_in(own_key, 6)
    for position, parts in cuts:
        heights = jnp.exp(jax.random.uniform(jax.random.fold_in(own, position), (parts,), jnp.float32, least / len(cuts), top_value / len(cuts)))
        loudness = loudness * jnp.repeat(heights, shape[position] // parts).reshape([-1 if axis == position else 1 for axis in range(len(shape))])
    return loudness


def centred(stream_key, extent, width, bound, cuts=(), kind=jnp.bfloat16):
    drawn = width * jax.random.normal(stream_key, extent, jnp.float32)
    if cuts:
        drawn = drawn * steps_of(stream_key, extent, cuts, -0.22, 0.18)
    return jnp.clip(drawn, -bound, bound).astype(kind)


def setup_inputs(seed: int = 0) -> dict:
    key_list = jax.random.split(jax.random.key(seed), 8)
    inputs = centred(key_list[0], (TOKENS, WR), 1.0, 6.0, ((0, 64),))
    out_grad = draw_out_grad(jax.random.fold_in(key_list[7], 71), 0)
    left_stat = draw_left_stat(jax.random.fold_in(key_list[7], 71), 0)
    right_stat = draw_right_stat(jax.random.fold_in(key_list[7], 71), 0)
    left_root = draw_left_root(jax.random.fold_in(key_list[7], 71), 0)
    right_root = draw_right_root(jax.random.fold_in(key_list[7], 71), 0)
    owner_blocks = draw_owner_blocks(jax.random.fold_in(key_list[7], 71), 0)
    return dict(inputs=inputs, out_grad=out_grad, left_stat=left_stat, right_stat=right_stat, left_root=left_root, right_root=right_root, owner_blocks=owner_blocks)


FACTOR_DECAY = 0.9
GRAFT_EPSILON = 1e-06

def reference(inputs, out_grad, left_stat, right_stat, left_root, right_root, owner_blocks):
    grad = jnp.dot(inputs.T, out_grad, preferred_element_type=jnp.float32)
    blocks = grad.reshape(RB, BLK, N_TENSOR, CBD, BLK).transpose(2, 0, 3, 1, 4).reshape(NB, BLK, BLK)
    padded = jnp.concatenate([blocks, jnp.zeros((1, BLK, BLK), blocks.dtype)], 0)
    slot_blocks = owner_blocks.reshape(-1).astype(jnp.int32)
    fraction = (1.0 - FACTOR_DECAY) / BLK

    def one_slot(values):
        slot_index, left_previous, right_old, left_inv, right_inv = values
        block_grad = padded[slot_index]
        left_gram_matrix = jnp.dot(block_grad, block_grad.T, preferred_element_type=jnp.float32, precision=lax.Precision.HIGHEST)
        right_gram = jnp.dot(block_grad.T, block_grad, preferred_element_type=jnp.float32, precision=lax.Precision.HIGHEST)
        left_upd = FACTOR_DECAY * left_previous + fraction * left_gram_matrix
        right_upd = FACTOR_DECAY * right_old + fraction * right_gram
        turned = jnp.dot(block_grad, right_inv, preferred_element_type=jnp.float32, precision=lax.Precision.HIGHEST)
        precond = jnp.dot(left_inv, turned, preferred_element_type=jnp.float32, precision=lax.Precision.HIGHEST)
        graft_scale = jnp.sqrt((jnp.mean(block_grad * block_grad) + GRAFT_EPSILON) / (jnp.mean(precond * precond) + GRAFT_EPSILON))
        return (left_upd, right_upd, (precond * graft_scale).astype(jnp.bfloat16))
    left_new, right_new, updates = lax.map(one_slot, (slot_blocks, left_stat, right_stat, left_root, right_root))
    slot_of_block = jnp.zeros((NB + 1,), jnp.int32).at[slot_blocks].set(jnp.arange(SLOTS, dtype=jnp.int32))[:NB]
    chosen = updates[slot_of_block]
    direction = chosen.reshape(N_TENSOR, RB, CBD, BLK, BLK).transpose(1, 3, 0, 2, 4).reshape(WR, WC)
    return (left_new, right_new, direction)
```

```python
import functools

import jax
import jax.numpy as jnp
from jax import lax
from jax.experimental import pallas as pl
from jax.experimental.pallas import tpu as pltpu
from jax.sharding import PartitionSpec as P

BLK = 512
NX = 4
NY = 4
NZ = 16
NT = 8
NB = 32
FACTOR_DECAY = 0.9
GRAFT_EPSILON = 1e-06
MESH = pl.DeviceIdType.MESH
F32 = jnp.float32
BF16 = jnp.bfloat16

NN = (((1,), (0,)), ((), ()))
NTR = (((1,), (1,)), ((), ()))
TN = (((0,), (0,)), ((), ()))


def dot(a, b, dims):
    return lax.dot_general(a, b, dims, preferred_element_type=F32)


def split(a):
    hi = a.astype(BF16)
    return hi, (a - hi.astype(F32)).astype(BF16)


def dot3(a, b, dims):
    return dot(a[0], b[0], dims) + (dot(a[0], b[1], dims) + dot(a[1], b[0], dims))


def loop(low, high, body):
    def step(k, carry):
        body(k)
        return carry

    lax.fori_loop(low, high, step, 0)


def kernel(
    x_ref, g_ref, ls_ref, rs_ref, lr_ref, rr_ref, ob_ref,
    ln_ref, rn_ref, dir_ref,
    xown, xb1, xb2, xb3, gown, gb1, gb2, gb3, part, ring_m, ring_p, own, r1, sb, hrel, lh, rrb, hhi, hlo, lsv, rsv, lgram,
    sq, sq_own, upd, fbuf, sb2, gr, zsel, xsel,
    loc, xs, xr, ys, yr, ds_, dr, gs, gr_s, lsd, lrv, rrs, rrr,
    rms, rmr, rps, rpr, a_s, a_r, b_s, b_r, c_s, c_r, cd_s, cd_r, e_s, e_r, f_s, f_r, h_s, h_r,
):
    d = lax.axis_index("dp")
    t = lax.axis_index("tensor")
    x = d // NZ
    z = d % NZ
    y = t // 2
    c = t % 2
    sib = y * 2 + (1 - c)

    def rc(src, dst, ssem, rsem, dx, dz, dt):
        return pltpu.make_async_remote_copy(
            src_ref=src, dst_ref=dst, send_sem=ssem, recv_sem=rsem,
            device_id=(dx * NZ + dz, dt), device_id_type=MESH,
        )

    local = [
        pltpu.make_async_copy(x_ref, xown, loc.at[0]),
        pltpu.make_async_copy(g_ref.at[:, pl.ds(pl.multiple_of(x * 128, 128), 128)], gown.at[0], loc.at[1]),
        pltpu.make_async_copy(g_ref.at[:, pl.ds(pl.multiple_of(512 + x * 128, 128), 128)], gown.at[1], loc.at[2]),
        pltpu.make_async_copy(rr_ref.at[0], rrb.at[c], loc.at[3]),
        pltpu.make_async_copy(ls_ref.at[0], lsv, loc.at[4]),
        pltpu.make_async_copy(rs_ref.at[0], rsv, loc.at[5]),
    ]
    for copy in local:
        copy.start()

    barrier = pltpu.get_barrier_semaphore()

    def greet_slab(k):
        pl.semaphore_signal(
            barrier, inc=1, device_id=(((x + k // NT) % NX) * NZ + z, (t + k % NT) % NT), device_id_type=MESH
        )

    def greet_ring(k):
        pl.semaphore_signal(barrier, inc=1, device_id=(x * NZ + (z + k) % NZ, t), device_id_type=MESH)

    loop(1, NX * NT, greet_slab)
    loop(1, NZ, greet_ring)
    pl.semaphore_wait(barrier, NX * NT - 1 + NZ - 1)

    order = (1, 3, 2)
    xb = (xown, xb1, xb2, xb3)
    gb = (gown, gb1, gb2, gb3)

    def x_copy(i):
        return rc(x_ref.at[y, c], xb[NX - i].at[0, 0], xs.at[i], xr.at[NX - i], (x + i) % NX, z, t)

    def g_copy(cb, i):
        to = (x + i) % NX
        columns = pl.ds(pl.multiple_of(cb * BLK + to * 128, 128), 128)
        return rc(g_ref.at[:, columns], gb[NX - i].at[cb], gs.at[cb, i], gr_s.at[cb, NX - i], to, z, t)

    x_send = [x_copy(i) for i in order]
    g_send = [g_copy(cb, i) for cb in range(2) for i in order]
    for copy in x_send + g_send:
        copy.start()

    rr_send = rc(rr_ref.at[0], rrb.at[c], rrs, rrr, x, z, sib)
    rr_send.start()
    l_core = y // 2
    l_self = l_core == c
    l_local = pltpu.make_async_copy(lr_ref.at[0], lh.at[t % 4], loc.at[6])

    def l_send(j):
        return rc(lr_ref.at[0], lh.at[t % 4], lsd.at[j], lrv.at[t % 4], x, z, ((y + j) % NY) * 2 + l_core)

    pl.when(l_self)(lambda: l_local.start())
    pl.when(jnp.logical_not(l_self))(lambda: l_send(0).start())
    for j in range(1, NY):
        l_send(j).start()

    def y_copy(i, j):
        to = ((y + j) % NY) * 2 + c
        return rc(xb[i].at[0, 0], xb[i].at[NY - j, 0], ys.at[i, j], yr.at[i, NY - j], x, z, to)

    def core_copy(i, j):
        return rc(xb[i].at[j, 0], xb[i].at[j, 1], ds_.at[i, j], dr.at[i, j], x, z, sib)

    y_send, d_send = [], []
    for i in order:
        x_copy(NX - i).wait_recv()
        for j in order:
            y_send.append(y_copy(i, j))
            y_send[-1].start()
        d_send.append(core_copy(i, 0))
        d_send[-1].start()

    def find_z(b):
        def step(k, found):
            return jnp.where(ob_ref[x * NZ + k] == b, k, found)

        zsel[b] = lax.fori_loop(0, NZ, step, 0)

    loop(0, NB, find_z)
    for cb in range(2):
        wanted = t * 4 + (x // 2) * 2 + cb

        def step(k, found):
            return jnp.where(ob_ref[k] == wanted, k // NZ, found)

        xsel[cb] = lax.fori_loop(0, NX * NZ, step, 0)

    for copy in local[:3]:
        copy.wait()

    def gram(act, grads):
        return [dot(grads[cb], act, TN).reshape(NZ, 8, 1024) for cb in range(2)]

    for cb, value in enumerate(gram(xown[...].reshape(256, 1024), gown)):
        part[cb] = value

    for i in order:
        for j in (3, 1, 2):
            y_copy(i, NY - j).wait_recv()
            d_send.append(core_copy(i, j))
            d_send[-1].start()
    for i in order:
        for j in range(NY):
            core_copy(i, j).wait_recv()
        for cb in range(2):
            g_copy(cb, NX - i).wait_recv()
        act = jnp.concatenate(
            [xb[i][(row + NY - y) % NY, (core + c) % 2] for row in range(NY) for core in range(2)], axis=0
        )
        for cb, value in enumerate(gram(act, gb[i])):
            part[cb] += value

    up, down = (z + 1) % NZ, (z + NZ - 1) % NZ

    def minus(cb, s, src):
        return rc(src, ring_m.at[cb, s], rms.at[cb, s], rmr.at[cb, s], x, down, t)

    def plus(cb, s, src):
        return rc(src, ring_p.at[cb, s], rps.at[cb, s], rpr.at[cb, s], x, up, t)

    for cb in range(2):
        minus(cb, 0, part.at[cb, (z + 8) % NZ]).start()
        plus(cb, 0, part.at[cb, (z + 7) % NZ]).start()

    for s in range(1, 8):
        for cb in range(2):
            minus(cb, s - 1, part.at[cb, 0]).wait_recv()
            ring_m[cb, s - 1] = ring_m[cb, s - 1] + part[cb, (z + 8 + s) % NZ]
            minus(cb, s, ring_m.at[cb, s - 1]).start()
            if s < 7:
                plus(cb, s - 1, part.at[cb, 0]).wait_recv()
                ring_p[cb, s - 1] = ring_p[cb, s - 1] + part[cb, (z + 7 - s) % NZ]
                plus(cb, s, ring_p.at[cb, s - 1]).start()
    for cb in range(2):
        plus(cb, 6, part.at[cb, 0]).wait_recv()
        minus(cb, 7, part.at[cb, 0]).wait_recv()
        total = part[cb, z] + (ring_p[cb, 6] + ring_m[cb, 7])
        for rb in range(2):
            for row in range(NY):
                low = rb * BLK + row * 128
                own[row, rb, cb] = total[:, low : low + 128]

    a_core = x // 2

    def a_copy(k):
        to_x, to_y = (x + k // NY) % NX, (y + k % NY) % NY
        return own.at[to_y], to_x, to_y * 2 + a_core

    def a_send(k):
        src, to_x, to_t = a_copy(k)
        return rc(src, r1.at[t, x % 2], a_s.at[k], a_r.at[t, x % 2], to_x, z, to_t)

    a_local = pltpu.make_async_copy(a_copy(0)[0], r1.at[t, x % 2], loc.at[7])
    a_self = a_core == c
    pl.when(a_self)(lambda: a_local.start())
    pl.when(jnp.logical_not(a_self))(lambda: a_send(0).start())
    loop(1, 16, lambda k: a_send(k).start())
    pl.when(a_self)(lambda: a_local.wait())

    def a_wait(k):
        from_t, half = k // 2, k % 2
        from_x = c * 2 + half

        @pl.when(jnp.logical_or(from_t != t, from_x != x))
        def _():
            piece = r1.at[from_t, half]
            rc(piece, piece, a_s.at[0], a_r.at[from_t, half], from_x, z, from_t).wait_recv()

    loop(0, 16, a_wait)

    def b_fill(k):
        block = ob_ref[x * NZ + k]
        safe = jnp.minimum(block, NB - 1)
        for half in range(2):
            value = r1[safe // 4, half, (safe // 2) % 2, safe % 2]
            sb[k, half] = jnp.where(block < NB, value, jnp.zeros_like(value))

    def b_send(k):
        to = (z + k) % NZ
        return rc(sb.at[to], hrel.at[0, 0, z], b_s.at[k], b_r.at[z], x, to, t)

    loop(0, NZ, b_fill)
    loop(1, NZ, lambda k: b_send(k).start())
    b_local = pltpu.make_async_copy(sb.at[z], hrel.at[0, 0, z], loc.at[9])
    b_local.start()

    def b_wait(k):
        src = (z + k) % NZ
        rc(sb.at[0], hrel.at[0, 0, src], b_s.at[0], b_r.at[src], x, src, t).wait_recv()

    loop(1, NZ, b_wait)
    b_local.wait()

    def c_copy(j):
        return rc(
            hrel.at[0, 0], hrel.at[0, NY - j], c_s.at[j], c_r.at[NY - j], x, z, ((y + j) % NY) * 2 + c
        )

    def cd_copy(j):
        return rc(hrel.at[0, j], hrel.at[1, j], cd_s.at[j], cd_r.at[j], x, z, sib)

    c_send = [c_copy(j) for j in order]
    for copy in c_send:
        copy.start()
    cd_send = [cd_copy(j) for j in (0, 1, 3, 2)]
    for j, copy in zip((0, 1, 3, 2), cd_send):
        if j > 0:
            c_copy(NY - j).wait_recv()
        copy.start()
    for copy in cd_send:
        copy.wait_recv()

    local[3].wait()
    rc(rrb.at[1 - c], rrb.at[1 - c], rrs, rrr, x, z, sib).wait_recv()
    pl.when(l_self)(lambda: l_local.wait())

    def l_wait(k):
        from_t = c * 4 + k

        @pl.when(from_t != t)
        def _():
            rc(lh.at[k], lh.at[k], lsd.at[0], lrv.at[k], x, z, from_t).wait_recv()

    loop(0, 4, l_wait)
    h = jnp.concatenate(
        [
            jnp.concatenate([hrel[(half // 2 + c) % 2, (row + NY - y) % NY, :, half % 2].reshape(128, 128) for half in range(NX)], axis=0)
            for row in range(NY)
        ],
        axis=1,
    )
    hi, lo = split(h)
    hhi[...] = hi
    hlo[...] = lo
    grad_square = jnp.sum(h * h) / (BLK * BLK)
    h2 = (hi, lo)
    turned = dot3(split(rrb[...].reshape(128, BLK)), h2, NN)
    precond = dot3(split(lh[...].reshape(256, BLK)), split(turned), NTR)
    sq_own[...] = jnp.sum((precond * precond).reshape(32, 8, 128), axis=0)

    def e_copy(k):
        return rc(sq_own, sq.at[NT - 1 - k], e_s.at[k], e_r.at[NT - k], x, z, (t + k) % NT)

    for k in range(1, NT):
        e_copy(k).start()

    fraction = (1.0 - FACTOR_DECAY) / BLK
    rows = pl.ds(pl.multiple_of(t * 64, 64), 64)
    local[5].wait()
    right = dot3((hhi[rows, :], hlo[rows, :]), h2, NTR)
    rn_ref[0] = FACTOR_DECAY * rsv[...] + fraction * right

    for k in range(1, NT):
        e_copy(k).wait_recv()
    prec_square = (jnp.sum(sq[...]) + jnp.sum(sq_own[...])) / (BLK * BLK)
    graft = jnp.sqrt(jnp.full((1, 128), (grad_square + GRAFT_EPSILON) / (prec_square + GRAFT_EPSILON), F32))
    upd[...] = (precond * graft).astype(BF16).reshape(NZ, 16, 128)

    def f_send(k):
        to = (z + k) % NZ
        return rc(upd.at[to], fbuf.at[z], f_s.at[k], f_r.at[z], x, to, t)

    loop(1, NZ, lambda k: f_send(k).start())
    f_local = pltpu.make_async_copy(upd.at[z], fbuf.at[z], loc.at[10])
    f_local.start()

    local[4].wait()
    lanes = pl.ds(pl.multiple_of(y * 128, 128), 128)
    left = dot3((hhi[:, lanes], hlo[:, lanes]), h2, TN)
    lgram[...] = left.reshape(2, 64, BLK)
    ln_ref[0] = FACTOR_DECAY * lsv[...] + fraction * lgram[c]

    def f_wait(k):
        src = (z + k) % NZ
        rc(fbuf.at[src], fbuf.at[src], f_s.at[k], f_r.at[src], x, src, t).wait_recv()

    loop(1, NZ, f_wait)
    f_local.wait()

    def h_fill(k):
        rb, to_t = k // NT, k % NT
        for cb in range(2):
            sb2[k, cb] = fbuf[zsel[to_t * 4 + rb * 2 + cb]]

    def h_is_self(k):
        return jnp.logical_and(c + 2 * (k // NT) == x, k % NT == t)

    def h_send(k):
        return rc(sb2.at[k], gr.at[x, y], h_s.at[k], h_r.at[x, y], c + 2 * (k // NT), z, k % NT)

    def h_start(k):
        pl.when(h_is_self(k))(lambda: pltpu.make_async_copy(sb2.at[k], gr.at[x, y], loc.at[8]).start())
        pl.when(jnp.logical_not(h_is_self(k)))(lambda: h_send(k).start())

    loop(0, 16, h_fill)
    loop(0, 16, h_start)

    def h_wait(k):
        from_x, from_y = k // NY, k % NY
        from_t = from_y * 2 + x % 2
        same = jnp.logical_and(from_x == x, from_t == t)
        place = gr.at[from_x, from_y]
        pl.when(same)(lambda: pltpu.make_async_copy(place, place, loc.at[8]).wait())
        pl.when(jnp.logical_not(same))(
            lambda: rc(place, place, h_s.at[0], h_r.at[from_x, from_y], from_x, z, from_t).wait_recv()
        )

    loop(0, 16, h_wait)
    for cb in range(2):
        for row in range(NY):
            dir_ref[:, cb * BLK + row * 128 : cb * BLK + (row + 1) * 128] = gr[xsel[cb], row, cb]

    for copy in x_send + g_send + y_send + d_send + c_send + cd_send + [rr_send]:
        copy.wait_send()
    pl.when(jnp.logical_not(l_self))(lambda: l_send(0).wait_send())
    for j in range(1, NY):
        l_send(j).wait_send()

    for s in range(8):
        for cb in range(2):
            minus(cb, s, part.at[cb, 0]).wait_send()
            if s < 7:
                plus(cb, s, part.at[cb, 0]).wait_send()
    pl.when(jnp.logical_not(a_self))(lambda: a_send(0).wait_send())
    loop(1, 16, lambda k: a_send(k).wait_send())
    loop(1, NZ, lambda k: b_send(k).wait_send())
    for k in range(1, NT):
        e_copy(k).wait_send()
    loop(1, NZ, lambda k: f_send(k).wait_send())
    loop(0, 16, lambda k: pl.when(jnp.logical_not(h_is_self(k)))(lambda: h_send(k).wait_send()))


def on_device(inputs, out_grad, left_stat, right_stat, left_root, right_root, owner_blocks):
    anywhere = pl.BlockSpec(memory_space=pltpu.HBM)
    in_vmem = pl.BlockSpec(memory_space=pltpu.VMEM)
    dma = pltpu.SemaphoreType.DMA
    return pl.pallas_call(
        kernel,
        out_shape=(
            jax.ShapeDtypeStruct((1, 64, BLK), F32),
            jax.ShapeDtypeStruct((1, 64, BLK), F32),
            jax.ShapeDtypeStruct((16, 1024), BF16),
        ),
        in_specs=[anywhere] * 6 + [pl.BlockSpec(memory_space=pltpu.SMEM)],
        out_specs=(in_vmem, in_vmem, in_vmem),
        scratch_shapes=[
            pltpu.VMEM((NY, 2, 32, 1024), BF16),
            pltpu.VMEM((NY, 2, 32, 1024), BF16),
            pltpu.VMEM((NY, 2, 32, 1024), BF16),
            pltpu.VMEM((NY, 2, 32, 1024), BF16),
            pltpu.VMEM((2, 256, 128), BF16),
            pltpu.VMEM((2, 256, 128), BF16),
            pltpu.VMEM((2, 256, 128), BF16),
            pltpu.VMEM((2, 256, 128), BF16),
            pltpu.VMEM((2, NZ, 8, 1024), F32),
            pltpu.VMEM((2, 8, 8, 1024), F32),
            pltpu.VMEM((2, 7, 8, 1024), F32),
            pltpu.VMEM((NY, 2, 2, 8, 128), F32),
            pltpu.VMEM((NT, 2, 2, 2, 8, 128), F32),
            pltpu.VMEM((NZ, 2, 8, 128), F32),
            pltpu.VMEM((2, NY, NZ, 2, 8, 128), F32),
            pltpu.VMEM((4, 64, BLK), F32),
            pltpu.VMEM((2, 64, BLK), F32),
            pltpu.VMEM((BLK, BLK), BF16),
            pltpu.VMEM((BLK, BLK), BF16),
            pltpu.VMEM((64, BLK), F32),
            pltpu.VMEM((64, BLK), F32),
            pltpu.VMEM((2, 64, BLK), F32),
            pltpu.VMEM((NT - 1, 8, 128), F32),
            pltpu.VMEM((8, 128), F32),
            pltpu.VMEM((NZ, 16, 128), BF16),
            pltpu.VMEM((NZ, 16, 128), BF16),
            pltpu.VMEM((16, 2, 16, 128), BF16),
            pltpu.VMEM((NX, NY, 2, 16, 128), BF16),
            pltpu.SMEM((NB,), jnp.int32),
            pltpu.SMEM((2,), jnp.int32),
            dma((11,)),
            dma((4,)), dma((4,)),
            dma((4, 4)), dma((4, 4)),
            dma((4, 4)), dma((4, 4)),
            dma((2, 4)), dma((2, 4)),
            dma((4,)), dma((4,)),
            dma, dma,
            dma((2, 8)), dma((2, 8)), dma((2, 7)), dma((2, 7)),
            dma((16,)), dma((8, 2)),
            dma((16,)), dma((16,)),
            dma((4,)), dma((4,)), dma((4,)), dma((4,)),
            dma((8,)), dma((8,)),
            dma((16,)), dma((16,)),
            dma((16,)), dma((4, 4)),
        ],
        compiler_params=pltpu.CompilerParams(
            collective_id=0, has_side_effects=True, vmem_limit_bytes=40 * 1024 * 1024
        ),
        name="shampoo",
    )(
        inputs.reshape(NY, 2, 32, 1024), out_grad, left_stat, right_stat, left_root, right_root,
        owner_blocks.reshape(NX * NZ),
    )


def solution(mesh):
    placed = (
        P("dp", None),
        P("dp", "tensor"),
        P("dp", "tensor", None),
        P("dp", "tensor", None),
        P("dp", "tensor", None),
        P("dp", "tensor", None),
        P(),
    )
    return jax.shard_map(
        on_device,
        mesh=mesh,
        in_specs=placed,
        out_specs=(P("dp", "tensor", None), P("dp", "tensor", None), P("dp", "tensor")),
        check_vma=False,
    )
```

```python
import functools

import jax
import jax.numpy as jnp
from jax import lax
from jax.experimental import pallas as pl
from jax.experimental.pallas import tpu as pltpu
from jax.sharding import PartitionSpec as P

BLK = 512
NX = 4
NY = 4
NZ = 16
NT = 8
NB = 32
FACTOR_DECAY = 0.9
GRAFT_EPSILON = 1e-06
MESH = pl.DeviceIdType.MESH
F32 = jnp.float32
BF16 = jnp.bfloat16

NN = (((1,), (0,)), ((), ()))
NTR = (((1,), (1,)), ((), ()))
TN = (((0,), (0,)), ((), ()))


def dot(a, b, dims):
    return lax.dot_general(a, b, dims, preferred_element_type=F32)


def split(a):
    hi = a.astype(BF16)
    return hi, (a - hi.astype(F32)).astype(BF16)


def dot3(a, b, dims):
    return dot(a[0], b[0], dims) + (dot(a[0], b[1], dims) + dot(a[1], b[0], dims))


def loop(low, high, body):
    def step(k, carry):
        body(k)
        return carry

    lax.fori_loop(low, high, step, 0)


def kernel(
    x_ref, g_ref, ls_ref, rs_ref, lr_ref, rr_ref, ob_ref,
    ln_ref, rn_ref, dir_ref,
    xown, xb1, xb2, xb3, gown, gb1, gb2, gb3, part, ring_m, ring_p, own, r1, sb, hrel, lh, rrb, hhi, hlo, lsv, rsv, lgram,
    sq, sq_own, upd, fbuf, sb2, gr, zsel, xsel,
    loc, xs, xr, ys, yr, ds_, dr, gs, gr_s, lsd, lrv, rrs, rrr,
    rms, rmr, rps, rpr, a_s, a_r, b_s, b_r, c_s, c_r, cd_s, cd_r, e_s, e_r, f_s, f_r, h_s, h_r,
):
    d = lax.axis_index("dp")
    t = lax.axis_index("tensor")
    x = d // NZ
    z = d % NZ
    y = t // 2
    c = t % 2
    sib = y * 2 + (1 - c)

    def rc(src, dst, ssem, rsem, dx, dz, dt):
        return pltpu.make_async_remote_copy(
            src_ref=src, dst_ref=dst, send_sem=ssem, recv_sem=rsem,
            device_id=(dx * NZ + dz, dt), device_id_type=MESH,
        )

    local = [
        pltpu.make_async_copy(x_ref, xown, loc.at[0]),
        pltpu.make_async_copy(g_ref.at[:, pl.ds(pl.multiple_of(x * 128, 128), 128)], gown.at[0], loc.at[1]),
        pltpu.make_async_copy(g_ref.at[:, pl.ds(pl.multiple_of(512 + x * 128, 128), 128)], gown.at[1], loc.at[2]),
        pltpu.make_async_copy(rr_ref.at[0], rrb.at[c], loc.at[3]),
        pltpu.make_async_copy(ls_ref.at[0], lsv, loc.at[4]),
        pltpu.make_async_copy(rs_ref.at[0], rsv, loc.at[5]),
    ]
    for copy in local:
        copy.start()

    barrier = pltpu.get_barrier_semaphore()
    met = [((x + i) % NX, z, t) for i in (1, 3, 2)] + [(x, z, (t + k) % NT) for k in range(1, NT)]
    met += [(x, (z + k) % NZ, t) for k in (1, NZ - 1)]
    for to_x, to_z, to_t in met:
        pl.semaphore_signal(barrier, inc=1, device_id=(to_x * NZ + to_z, to_t), device_id_type=MESH)
    pl.semaphore_wait(barrier, len(met))

    order = (1, 3, 2)
    xb = (xown, xb1, xb2, xb3)
    gb = (gown, gb1, gb2, gb3)

    def x_copy(i, j):
        src = x_ref.at[(y + j) % NY, c]
        return rc(src, xb[NX - i].at[j, 0], xs.at[i, j], xr.at[NX - i, j], (x + i) % NX, z, t)

    def g_copy(cb, i):
        to = (x + i) % NX
        columns = pl.ds(pl.multiple_of(cb * BLK + to * 128, 128), 128)
        return rc(g_ref.at[:, columns], gb[NX - i].at[cb], gs.at[cb, i], gr_s.at[cb, NX - i], to, z, t)

    x_send = [x_copy(i, j) for j in (0, 2) for i in order]
    g_send = [g_copy(cb, i) for cb in range(2) for i in order]
    for copy in x_send + g_send:
        copy.start()

    for copy in local[:3]:
        copy.wait()

    def gram(act, grads):
        value = dot(jnp.concatenate([grads[0], grads[1]], axis=1), act, TN)
        for cb in range(2):
            for rb in range(2):
                yield cb, rb, value[cb * 128 : cb * 128 + 128, rb * BLK : rb * BLK + BLK].reshape(NZ, 8, BLK)

    for cb, rb, value in gram(xown[...].reshape(256, 1024), gown):
        part[cb, rb] = value

    def y_copy(i, j):
        to = ((y + j) % NY) * 2 + c
        return rc(xb[i].at[0, 0], xb[i].at[NY - j, 0], ys.at[i, j], yr.at[i, NY - j], x, z, to)

    def core_copy(i, j):
        return rc(xb[i].at[j, 0], xb[i].at[j, 1], ds_.at[i, j], dr.at[i, j], x, z, sib)

    y_send, d_send = [], []
    for i in order:
        x_copy(NX - i, 0).wait_recv()
        for j in (1, 3):
            y_send.append(y_copy(i, j))
            y_send[-1].start()
        d_send.append(core_copy(i, 0))
        d_send[-1].start()

    for i in order:
        for j in (2, 1, 3):
            if j == 2:
                x_copy(NX - i, 2).wait_recv()
            else:
                y_copy(i, NY - j).wait_recv()
            d_send.append(core_copy(i, j))
            d_send[-1].start()
    for i in order:
        for j in range(NY):
            core_copy(i, j).wait_recv()
        for cb in range(2):
            g_copy(cb, NX - i).wait_recv()
        act = jnp.concatenate(
            [xb[i][(row + NY - y) % NY, (core + c) % 2] for row in range(NY) for core in range(2)], axis=0
        )
        for cb, rb, value in gram(act, gb[i]):
            part[cb, rb] += value

    up, down = (z + 1) % NZ, (z + NZ - 1) % NZ

    chunks = [(cb, rb) for cb in range(2) for rb in range(2)]

    def minus(q, s, src):
        return rc(src, ring_m.at[*q, s], rms.at[*q, s], rmr.at[*q, s], x, down, t)

    def plus(q, s, src):
        return rc(src, ring_p.at[*q, s], rps.at[*q, s], rpr.at[*q, s], x, up, t)

    for q in chunks:
        minus(q, 0, part.at[*q, (z + 8) % NZ]).start()
        plus(q, 0, part.at[*q, (z + 7) % NZ]).start()

    rr_send = rc(rr_ref.at[0], rrb.at[c], rrs, rrr, x, z, sib)
    rr_send.start()
    l_core = y // 2
    l_self = l_core == c
    l_local = pltpu.make_async_copy(lr_ref.at[0], lh.at[t % 4], loc.at[6])

    def l_send(j):
        return rc(lr_ref.at[0], lh.at[t % 4], lsd.at[j], lrv.at[t % 4], x, z, ((y + j) % NY) * 2 + l_core)

    pl.when(l_self)(lambda: l_local.start())
    pl.when(jnp.logical_not(l_self))(lambda: l_send(0).start())
    for j in range(1, NY):
        l_send(j).start()

    for s in range(1, 8):
        for q in chunks:
            minus(q, s - 1, part.at[*q, 0]).wait_recv()
            ring_m[*q, s - 1] = ring_m[*q, s - 1] + part[*q, (z + 8 + s) % NZ]
            minus(q, s, ring_m.at[*q, s - 1]).start()
            if s < 7:
                plus(q, s - 1, part.at[*q, 0]).wait_recv()
                ring_p[*q, s - 1] = ring_p[*q, s - 1] + part[*q, (z + 7 - s) % NZ]
                plus(q, s, ring_p.at[*q, s - 1]).start()
    for q in chunks:
        plus(q, 6, part.at[*q, 0]).wait_recv()
        minus(q, 7, part.at[*q, 0]).wait_recv()
        total = part[*q, z] + (ring_p[*q, 6] + ring_m[*q, 7])
        for row in range(NY):
            own[row, q[1], q[0]] = total[:, row * 128 : row * 128 + 128]

    a_core = x // 2

    def a_copy(k):
        to_x, to_y = (x + k // NY) % NX, (y + k % NY) % NY
        return own.at[to_y], to_x, to_y * 2 + a_core

    def a_send(k):
        src, to_x, to_t = a_copy(k)
        return rc(src, r1.at[t, x % 2], a_s.at[k], a_r.at[t, x % 2], to_x, z, to_t)

    a_local = pltpu.make_async_copy(a_copy(0)[0], r1.at[t, x % 2], loc.at[7])
    a_self = a_core == c
    pl.when(a_self)(lambda: a_local.start())
    pl.when(jnp.logical_not(a_self))(lambda: a_send(0).start())
    loop(1, 16, lambda k: a_send(k).start())
    pl.when(a_self)(lambda: a_local.wait())

    def a_wait(k):
        from_t, half = k // 2, k % 2
        from_x = c * 2 + half

        @pl.when(jnp.logical_or(from_t != t, from_x != x))
        def _():
            piece = r1.at[from_t, half]
            rc(piece, piece, a_s.at[0], a_r.at[from_t, half], from_x, z, from_t).wait_recv()

    loop(0, 16, a_wait)

    def slot_of(o):
        return max(2 * o - 1, 0) if o <= 8 else 2 * NZ - 2 * o

    offset_of = sorted(range(NZ), key=slot_of)

    def b_fill(k):
        block = ob_ref[x * NZ + k]
        safe = jnp.minimum(block, NB - 1)
        for half in range(2):
            value = r1[safe // 4, half, (safe // 2) % 2, safe % 2]
            sb[k, half] = jnp.where(block < NB, value, jnp.zeros_like(value))

    def b_copy(k):
        to = (z + k) % NZ
        return rc(sb.at[to], hrel.at[0, 0, slot_of(NZ - k)], b_s.at[k], b_r.at[NZ - k], x, to, t)

    loop(0, NZ, b_fill)
    b_local = pltpu.make_async_copy(sb.at[z], hrel.at[0, 0, 0], loc.at[9])
    b_local.start()
    for o in offset_of[:0:-1]:
        b_copy(NZ - o).start()

    def c_copy(g, j):
        src, dst = hrel.at[0, 0, pl.ds(4 * g, 4)], hrel.at[0, NY - j, pl.ds(4 * g, 4)]
        return rc(src, dst, c_s.at[g, j], c_r.at[g, NY - j], x, z, ((y + j) % NY) * 2 + c)

    def cd_copy(g, j):
        src, dst = hrel.at[0, j, pl.ds(4 * g, 4)], hrel.at[1, j, pl.ds(4 * g, 4)]
        return rc(src, dst, cd_s.at[g, j], cd_r.at[g, j], x, z, sib)

    c_send, cd_send = [], []

    def pass_on(g):
        for j in (1, 3, 2):
            c_copy(g, NY - j).wait_recv()
            cd_copy(g, j).start()
            cd_send.append(cd_copy(g, j))

    for g in range(4):
        for o in offset_of[4 * g : 4 * g + 4]:
            if o == 0:
                b_local.wait()
            else:
                b_copy(NZ - o).wait_recv()
        for j in (1, 3, 2):
            c_copy(g, j).start()
            c_send.append(c_copy(g, j))
        cd_copy(g, 0).start()
        cd_send.append(cd_copy(g, 0))
        if g > 0:
            pass_on(g - 1)
    pass_on(3)
    for copy in cd_send:
        copy.wait_recv()

    local[3].wait()
    rc(rrb.at[1 - c], rrb.at[1 - c], rrs, rrr, x, z, sib).wait_recv()
    pl.when(l_self)(lambda: l_local.wait())

    def l_wait(k):
        from_t = c * 4 + k

        @pl.when(from_t != t)
        def _():
            rc(lh.at[k], lh.at[k], lsd.at[0], lrv.at[k], x, z, from_t).wait_recv()

    loop(0, 4, l_wait)
    def place(row):
        o = (row + NZ - z) % NZ
        return jnp.where(o <= 8, jnp.maximum(2 * o - 1, 0), 2 * NZ - 2 * o)

    def tile(col_x, row_z, row):
        return hrel[(col_x // 2 + c) % 2, (row + NY - y) % NY, place(row_z), col_x % 2]

    h = jnp.concatenate(
        [
            jnp.concatenate([tile(col_x, row_z, row) for row in range(NY)], axis=1)
            for col_x in range(NX)
            for row_z in range(NZ)
        ],
        axis=0,
    )
    hi, lo = split(h)
    hhi[...] = hi
    hlo[...] = lo
    grad_square = jnp.sum(h * h) / (BLK * BLK)
    h2 = (hi, lo)
    turned = dot3(split(rrb[...].reshape(128, BLK)), h2, NN)
    precond = dot3(split(lh[...].reshape(256, BLK)), split(turned), NTR)
    sq_own[...] = jnp.sum((precond * precond).reshape(32, 8, 128), axis=0)

    def e_copy(k):
        return rc(sq_own, sq.at[NT - 1 - k], e_s.at[k], e_r.at[NT - k], x, z, (t + k) % NT)

    for k in range(1, NT):
        e_copy(k).start()

    fraction = (1.0 - FACTOR_DECAY) / BLK
    rows = pl.ds(pl.multiple_of(t * 64, 64), 64)
    local[5].wait()
    right = dot3((hhi[rows, :], hlo[rows, :]), h2, NTR)
    rn_ref[0] = FACTOR_DECAY * rsv[...] + fraction * right

    for k in range(1, NT):
        e_copy(k).wait_recv()
    prec_square = (jnp.sum(sq[...]) + jnp.sum(sq_own[...])) / (BLK * BLK)
    graft = jnp.sqrt(jnp.full((1, 128), (grad_square + GRAFT_EPSILON) / (prec_square + GRAFT_EPSILON), F32))
    upd[...] = (precond * graft).astype(BF16).reshape(NZ, 16, 128)

    def f_send(k):
        to = (z + k) % NZ
        return rc(upd.at[to], fbuf.at[z], f_s.at[k], f_r.at[z], x, to, t)

    loop(1, NZ, lambda k: f_send(k).start())
    f_local = pltpu.make_async_copy(upd.at[z], fbuf.at[z], loc.at[10])
    f_local.start()

    local[4].wait()
    lanes = pl.ds(pl.multiple_of(y * 128, 128), 128)
    left = dot3((hhi[:, lanes], hlo[:, lanes]), h2, TN)
    lgram[...] = left.reshape(2, 64, BLK)
    ln_ref[0] = FACTOR_DECAY * lsv[...] + fraction * lgram[c]

    def find_z(b):
        def step(k, found):
            return jnp.where(ob_ref[x * NZ + k] == b, k, found)

        zsel[b] = lax.fori_loop(0, NZ, step, 0)

    loop(0, NB, find_z)
    for cb in range(2):
        wanted = t * 4 + (x // 2) * 2 + cb

        def step(k, found):
            return jnp.where(ob_ref[k] == wanted, k // NZ, found)

        xsel[cb] = lax.fori_loop(0, NX * NZ, step, 0)

    def f_wait(k):
        src = (z + k) % NZ
        rc(fbuf.at[src], fbuf.at[src], f_s.at[k], f_r.at[src], x, src, t).wait_recv()

    loop(1, NZ, f_wait)
    f_local.wait()

    def h_fill(k):
        rb, to_t = k // NT, k % NT
        for cb in range(2):
            sb2[k, cb] = fbuf[zsel[to_t * 4 + rb * 2 + cb]]

    def h_is_self(k):
        return jnp.logical_and(c + 2 * (k // NT) == x, k % NT == t)

    def h_send(k):
        return rc(sb2.at[k], gr.at[x, y], h_s.at[k], h_r.at[x, y], c + 2 * (k // NT), z, k % NT)

    def h_start(k):
        pl.when(h_is_self(k))(lambda: pltpu.make_async_copy(sb2.at[k], gr.at[x, y], loc.at[8]).start())
        pl.when(jnp.logical_not(h_is_self(k)))(lambda: h_send(k).start())

    loop(0, 16, h_fill)
    loop(0, 16, h_start)

    def h_wait(k):
        from_x, from_y = k // NY, k % NY
        from_t = from_y * 2 + x % 2
        same = jnp.logical_and(from_x == x, from_t == t)
        place = gr.at[from_x, from_y]
        pl.when(same)(lambda: pltpu.make_async_copy(place, place, loc.at[8]).wait())
        pl.when(jnp.logical_not(same))(
            lambda: rc(place, place, h_s.at[0], h_r.at[from_x, from_y], from_x, z, from_t).wait_recv()
        )

    loop(0, 16, h_wait)
    for cb in range(2):
        for row in range(NY):
            dir_ref[:, cb * BLK + row * 128 : cb * BLK + (row + 1) * 128] = gr[xsel[cb], row, cb]

    for copy in x_send + g_send + y_send + d_send + c_send + cd_send + [rr_send]:
        copy.wait_send()
    pl.when(jnp.logical_not(l_self))(lambda: l_send(0).wait_send())
    for j in range(1, NY):
        l_send(j).wait_send()

    for s in range(8):
        for q in chunks:
            minus(q, s, part.at[*q, 0]).wait_send()
            if s < 7:
                plus(q, s, part.at[*q, 0]).wait_send()
    pl.when(jnp.logical_not(a_self))(lambda: a_send(0).wait_send())
    loop(1, 16, lambda k: a_send(k).wait_send())
    for k in range(1, NZ):
        b_copy(k).wait_send()
    for k in range(1, NT):
        e_copy(k).wait_send()
    loop(1, NZ, lambda k: f_send(k).wait_send())
    loop(0, 16, lambda k: pl.when(jnp.logical_not(h_is_self(k)))(lambda: h_send(k).wait_send()))


def on_device(inputs, out_grad, left_stat, right_stat, left_root, right_root, owner_blocks):
    anywhere = pl.BlockSpec(memory_space=pltpu.HBM)
    in_vmem = pl.BlockSpec(memory_space=pltpu.VMEM)
    dma = pltpu.SemaphoreType.DMA
    return pl.pallas_call(
        kernel,
        out_shape=(
            jax.ShapeDtypeStruct((1, 64, BLK), F32),
            jax.ShapeDtypeStruct((1, 64, BLK), F32),
            jax.ShapeDtypeStruct((16, 1024), BF16),
        ),
        in_specs=[anywhere] * 6 + [pl.BlockSpec(memory_space=pltpu.SMEM)],
        out_specs=(in_vmem, in_vmem, in_vmem),
        scratch_shapes=[
            pltpu.VMEM((NY, 2, 32, 1024), BF16),
            pltpu.VMEM((NY, 2, 32, 1024), BF16),
            pltpu.VMEM((NY, 2, 32, 1024), BF16),
            pltpu.VMEM((NY, 2, 32, 1024), BF16),
            pltpu.VMEM((2, 256, 128), BF16),
            pltpu.VMEM((2, 256, 128), BF16),
            pltpu.VMEM((2, 256, 128), BF16),
            pltpu.VMEM((2, 256, 128), BF16),
            pltpu.VMEM((2, 2, NZ, 8, BLK), F32),
            pltpu.VMEM((2, 2, 8, 8, BLK), F32),
            pltpu.VMEM((2, 2, 7, 8, BLK), F32),
            pltpu.VMEM((NY, 2, 2, 8, 128), F32),
            pltpu.VMEM((NT, 2, 2, 2, 8, 128), F32),
            pltpu.VMEM((NZ, 2, 8, 128), F32),
            pltpu.VMEM((2, NY, NZ, 2, 8, 128), F32),
            pltpu.VMEM((4, 64, BLK), F32),
            pltpu.VMEM((2, 64, BLK), F32),
            pltpu.VMEM((BLK, BLK), BF16),
            pltpu.VMEM((BLK, BLK), BF16),
            pltpu.VMEM((64, BLK), F32),
            pltpu.VMEM((64, BLK), F32),
            pltpu.VMEM((2, 64, BLK), F32),
            pltpu.VMEM((NT - 1, 8, 128), F32),
            pltpu.VMEM((8, 128), F32),
            pltpu.VMEM((NZ, 16, 128), BF16),
            pltpu.VMEM((NZ, 16, 128), BF16),
            pltpu.VMEM((16, 2, 16, 128), BF16),
            pltpu.VMEM((NX, NY, 2, 16, 128), BF16),
            pltpu.SMEM((NB,), jnp.int32),
            pltpu.SMEM((2,), jnp.int32),
            dma((11,)),
            dma((4, 4)), dma((4, 4)),
            dma((4, 4)), dma((4, 4)),
            dma((4, 4)), dma((4, 4)),
            dma((2, 4)), dma((2, 4)),
            dma((4,)), dma((4,)),
            dma, dma,
            dma((2, 2, 8)), dma((2, 2, 8)), dma((2, 2, 7)), dma((2, 2, 7)),
            dma((16,)), dma((8, 2)),
            dma((16,)), dma((16,)),
            dma((4, 4)), dma((4, 4)), dma((4, 4)), dma((4, 4)),
            dma((8,)), dma((8,)),
            dma((16,)), dma((16,)),
            dma((16,)), dma((4, 4)),
        ],
        compiler_params=pltpu.CompilerParams(
            collective_id=0, has_side_effects=True, vmem_limit_bytes=63 * 1024 * 1024 + 900 * 1024
        ),
        name="shampoo",
    )(
        inputs.reshape(NY, 2, 32, 1024), out_grad, left_stat, right_stat, left_root, right_root,
        owner_blocks.reshape(NX * NZ),
    )


def solution(mesh):
    placed = (
        P("dp", None),
        P("dp", "tensor"),
        P("dp", "tensor", None),
        P("dp", "tensor", None),
        P("dp", "tensor", None),
        P("dp", "tensor", None),
        P(),
    )
    return jax.shard_map(
        on_device,
        mesh=mesh,
        in_specs=placed,
        out_specs=(P("dp", "tensor", None), P("dp", "tensor", None), P("dp", "tensor")),
        check_vma=False,
    )
```

```python
import functools

import jax
import jax.numpy as jnp
from jax import lax
from jax.experimental import pallas as pl
from jax.experimental.pallas import tpu as pltpu
from jax.sharding import PartitionSpec as P

BLK = 512
NX = 4
NY = 4
NZ = 16
NT = 8
NB = 32
FACTOR_DECAY = 0.9
GRAFT_EPSILON = 1e-06
MESH = pl.DeviceIdType.MESH
F32 = jnp.float32
BF16 = jnp.bfloat16

NN = (((1,), (0,)), ((), ()))
NTR = (((1,), (1,)), ((), ()))
TN = (((0,), (0,)), ((), ()))


def dot(a, b, dims):
    return lax.dot_general(a, b, dims, preferred_element_type=F32)


def split(a):
    hi = a.astype(BF16)
    return hi, (a - hi.astype(F32)).astype(BF16)


def dot3(a, b, dims):
    return dot(a[0], b[0], dims) + (dot(a[0], b[1], dims) + dot(a[1], b[0], dims))


def loop(low, high, body):
    def step(k, carry):
        body(k)
        return carry

    lax.fori_loop(low, high, step, 0)


def kernel(
    x_ref, g_ref, ls_ref, rs_ref, lr_ref, rr_ref, ob_ref,
    ln_ref, rn_ref, dir_ref,
    xown, xb1, xb2, xb3, gown, gb1, gb2, gb3, part, ring_1, ring_2, ring_a, own, r1, sb, hrel, lh, rrb, hhi, hlo, lsv, rsv, lgram,
    sq, sq_own, upd, fbuf, sb2, gr, zsel, xsel,
    loc, xs, xr, ys, yr, ds_, dr, gs, gr_s, lsd, lrv, rrs, rrr,
    r1s, r1r, r2s, r2r, a_s, a_r, b_s, b_r, c_s, c_r, cd_s, cd_r, e_s, e_r, f_s, f_r, h_s, h_r,
):
    d = lax.axis_index("dp")
    t = lax.axis_index("tensor")
    x = d // NZ
    z = d % NZ
    y = t // 2
    c = t % 2
    sib = y * 2 + (1 - c)

    def rc(src, dst, ssem, rsem, dx, dz, dt):
        return pltpu.make_async_remote_copy(
            src_ref=src, dst_ref=dst, send_sem=ssem, recv_sem=rsem,
            device_id=(dx * NZ + dz, dt), device_id_type=MESH,
        )

    local = [
        pltpu.make_async_copy(x_ref, xown, loc.at[0]),
        pltpu.make_async_copy(g_ref.at[:, pl.ds(pl.multiple_of(x * 128, 128), 128)], gown.at[0], loc.at[1]),
        pltpu.make_async_copy(g_ref.at[:, pl.ds(pl.multiple_of(512 + x * 128, 128), 128)], gown.at[1], loc.at[2]),
        pltpu.make_async_copy(rr_ref.at[0], rrb.at[c], loc.at[3]),
        pltpu.make_async_copy(ls_ref.at[0], lsv, loc.at[4]),
        pltpu.make_async_copy(rs_ref.at[0], rsv, loc.at[5]),
    ]
    for copy in local:
        copy.start()

    barrier = pltpu.get_barrier_semaphore()
    met = [((x + i) % NX, z, t) for i in (1, 3, 2)] + [(x, z, (t + k) % NT) for k in range(1, NT)]
    met += [(x, (z + k) % NZ, t) for k in (1, NZ - 1, 2, NZ - 2)]
    for to_x, to_z, to_t in met:
        pl.semaphore_signal(barrier, inc=1, device_id=(to_x * NZ + to_z, to_t), device_id_type=MESH)
    pl.semaphore_wait(barrier, len(met))

    order = (1, 3, 2)
    xb = (xown, xb1, xb2, xb3)
    gb = (gown, gb1, gb2, gb3)

    def x_copy(i, j):
        src = x_ref.at[(y + j) % NY, c]
        return rc(src, xb[NX - i].at[j, 0], xs.at[i, j], xr.at[NX - i, j], (x + i) % NX, z, t)

    def g_copy(cb, i):
        to = (x + i) % NX
        columns = pl.ds(pl.multiple_of(cb * BLK + to * 128, 128), 128)
        return rc(g_ref.at[:, columns], gb[NX - i].at[cb], gs.at[cb, i], gr_s.at[cb, NX - i], to, z, t)

    x_send = [x_copy(i, j) for j in (0, 2) for i in order]
    g_send = [g_copy(cb, i) for cb in range(2) for i in order]
    for copy in x_send + g_send:
        copy.start()

    for copy in local[:3]:
        copy.wait()

    def gram(act, grads):
        value = dot(jnp.concatenate([grads[0], grads[1]], axis=1), act, TN)
        for cb in range(2):
            for rb in range(2):
                yield cb, rb, value[cb * 128 : cb * 128 + 128, rb * BLK : rb * BLK + BLK].reshape(NZ, 8, BLK)

    for cb, rb, value in gram(xown[...].reshape(256, 1024), gown):
        part[cb, rb] = value

    def y_copy(i, j):
        to = ((y + j) % NY) * 2 + c
        return rc(xb[i].at[0, 0], xb[i].at[NY - j, 0], ys.at[i, j], yr.at[i, NY - j], x, z, to)

    def core_copy(i, j):
        return rc(xb[i].at[j, 0], xb[i].at[j, 1], ds_.at[i, j], dr.at[i, j], x, z, sib)

    y_send, d_send = [], []
    for i in order:
        x_copy(NX - i, 0).wait_recv()
        for j in (1, 3):
            y_send.append(y_copy(i, j))
            y_send[-1].start()
        d_send.append(core_copy(i, 0))
        d_send[-1].start()

    for i in order:
        for j in (2, 1, 3):
            if j == 2:
                x_copy(NX - i, 2).wait_recv()
            else:
                y_copy(i, NY - j).wait_recv()
            d_send.append(core_copy(i, j))
            d_send[-1].start()
    for i in order:
        for j in range(NY):
            core_copy(i, j).wait_recv()
        for cb in range(2):
            g_copy(cb, NX - i).wait_recv()
        act = jnp.concatenate(
            [xb[i][(row + NY - y) % NY, (core + c) % 2] for row in range(NY) for core in range(2)], axis=0
        )
        for cb, rb, value in gram(act, gb[i]):
            part[cb, rb] += value

    chunks = [(cb, rb) for cb in range(2) for rb in range(2)]
    ways = (-1, 1)

    def ring_to(way, far):
        return (z + NZ + way * far) % NZ

    def one(q, way, m, src=None):
        w = (way + 1) // 2
        src = part.at[*q, 0] if src is None else src
        k = m // 2
        return rc(src, ring_1.at[w, *q, k], r1s.at[w, *q, k], r1r.at[w, *q, k], x, ring_to(way, 1), t)

    def two(q, way, m, src=None):
        w = (way + 1) // 2
        src = part.at[*q, 0] if src is None else src
        k = m // 2 - 1
        return rc(src, ring_2.at[w, *q, k], r2s.at[w, *q, k], r2r.at[w, *q, k], x, ring_to(way, 2), t)

    def ring_one(m):
        for q in chunks:
            for way in ways:
                one(q, way, m, part.at[*q, ring_to(way, m)]).start()

    def gathered(q, way, m):
        w = (way + 1) // 2
        one(q, way, m + 1).wait_recv()
        total = ring_1[w, *q, m // 2]
        if m < (8 if way < 0 else 6) - 1:
            two(q, way, m + 2).wait_recv()
            total = total + ring_2[w, *q, m // 2]
        return total

    for q in chunks:
        two(q, -1, 8, part.at[*q, ring_to(-1, 8)]).start()
        for way in (1, -1):
            one(q, way, 7, part.at[*q, ring_to(way, 7)]).start()
    ring_one(5)
    rr_send = rc(rr_ref.at[0], rrb.at[c], rrs, rrr, x, z, sib)
    rr_send.start()
    l_core = y // 2
    l_self = l_core == c
    l_local = pltpu.make_async_copy(lr_ref.at[0], lh.at[t % 4], loc.at[6])

    def l_send(j):
        return rc(lr_ref.at[0], lh.at[t % 4], lsd.at[j], lrv.at[t % 4], x, z, ((y + j) % NY) * 2 + l_core)

    pl.when(l_self)(lambda: l_local.start())
    pl.when(jnp.logical_not(l_self))(lambda: l_send(0).start())
    for j in range(1, NY):
        l_send(j).start()

    for m in (6, 4, 2):
        for q in chunks:
            for way in ways:
                w = (way + 1) // 2
                ring_a[w, *q, m // 2 - 1] = part[*q, ring_to(way, m)] + gathered(q, way, m)
                two(q, way, m, ring_a.at[w, *q, m // 2 - 1]).start()
        if m > 2:
            ring_one(m - 3)
    for q in chunks:
        total = part[*q, z] + (gathered(q, -1, 0) + gathered(q, 1, 0))
        for row in range(NY):
            own[row, q[1], q[0]] = total[:, row * 128 : row * 128 + 128]

    a_core = x // 2

    def a_copy(k):
        to_x, to_y = (x + k // NY) % NX, (y + k % NY) % NY
        return own.at[to_y], to_x, to_y * 2 + a_core

    def a_send(k):
        src, to_x, to_t = a_copy(k)
        return rc(src, r1.at[t, x % 2], a_s.at[k], a_r.at[t, x % 2], to_x, z, to_t)

    a_local = pltpu.make_async_copy(a_copy(0)[0], r1.at[t, x % 2], loc.at[7])
    a_self = a_core == c
    pl.when(a_self)(lambda: a_local.start())
    pl.when(jnp.logical_not(a_self))(lambda: a_send(0).start())
    loop(1, 16, lambda k: a_send(k).start())
    pl.when(a_self)(lambda: a_local.wait())

    def a_wait(k):
        from_t, half = k // 2, k % 2
        from_x = c * 2 + half

        @pl.when(jnp.logical_or(from_t != t, from_x != x))
        def _():
            piece = r1.at[from_t, half]
            rc(piece, piece, a_s.at[0], a_r.at[from_t, half], from_x, z, from_t).wait_recv()

    loop(0, 16, a_wait)

    def slot_of(o):
        return max(2 * o - 1, 0) if o <= 8 else 2 * NZ - 2 * o

    offset_of = sorted(range(NZ), key=slot_of)

    def b_fill(k):
        block = ob_ref[x * NZ + (z + k) % NZ]
        safe = jnp.minimum(block, NB - 1)
        for half in range(2):
            value = r1[safe // 4, half, (safe // 2) % 2, safe % 2]
            sb[k, half] = jnp.where(block < NB, value, jnp.zeros_like(value))

    def b_copy(k):
        to = (z + k) % NZ
        return rc(sb.at[k], hrel.at[0, 0, slot_of(NZ - k)], b_s.at[k], b_r.at[NZ - k], x, to, t)

    b_local = pltpu.make_async_copy(sb.at[0], hrel.at[0, 0, 0], loc.at[9])
    for o in offset_of:
        b_fill(o)
        if o == 0:
            b_local.start()
        else:
            b_copy(o).start()

    def c_copy(g, j):
        src, dst = hrel.at[0, 0, pl.ds(4 * g, 4)], hrel.at[0, NY - j, pl.ds(4 * g, 4)]
        return rc(src, dst, c_s.at[g, j], c_r.at[g, NY - j], x, z, ((y + j) % NY) * 2 + c)

    def cd_copy(g, j):
        src, dst = hrel.at[0, j, pl.ds(4 * g, 4)], hrel.at[1, j, pl.ds(4 * g, 4)]
        return rc(src, dst, cd_s.at[g, j], cd_r.at[g, j], x, z, sib)

    c_send, cd_send = [], []

    def pass_on(g):
        for j in (1, 3, 2):
            c_copy(g, NY - j).wait_recv()
            cd_copy(g, j).start()
            cd_send.append(cd_copy(g, j))

    for g in range(4):
        for o in offset_of[4 * g : 4 * g + 4]:
            if o == 0:
                b_local.wait()
            else:
                b_copy(NZ - o).wait_recv()
        for j in (1, 3, 2):
            c_copy(g, j).start()
            c_send.append(c_copy(g, j))
        cd_copy(g, 0).start()
        cd_send.append(cd_copy(g, 0))
        if g > 0:
            pass_on(g - 1)
    pass_on(3)
    for copy in cd_send:
        copy.wait_recv()

    local[3].wait()
    rc(rrb.at[1 - c], rrb.at[1 - c], rrs, rrr, x, z, sib).wait_recv()
    pl.when(l_self)(lambda: l_local.wait())

    def l_wait(k):
        from_t = c * 4 + k

        @pl.when(from_t != t)
        def _():
            rc(lh.at[k], lh.at[k], lsd.at[0], lrv.at[k], x, z, from_t).wait_recv()

    loop(0, 4, l_wait)
    def place(row):
        o = (row + NZ - z) % NZ
        return jnp.where(o <= 8, jnp.maximum(2 * o - 1, 0), 2 * NZ - 2 * o)

    def tile(col_x, row_z, row):
        return hrel[(col_x // 2 + c) % 2, (row + NY - y) % NY, place(row_z), col_x % 2]

    h = jnp.concatenate(
        [
            jnp.concatenate([tile(col_x, row_z, row) for row in range(NY)], axis=1)
            for col_x in range(NX)
            for row_z in range(NZ)
        ],
        axis=0,
    )
    hi, lo = split(h)
    hhi[...] = hi
    hlo[...] = lo
    grad_square = jnp.sum(h * h) / (BLK * BLK)
    h2 = (hi, lo)
    turned = dot3(split(rrb[...].reshape(128, BLK)), h2, NN)
    precond = dot3(split(lh[...].reshape(256, BLK)), split(turned), NTR)
    sq_own[...] = jnp.sum((precond * precond).reshape(32, 8, 128), axis=0)

    def e_copy(k):
        return rc(sq_own, sq.at[NT - 1 - k], e_s.at[k], e_r.at[NT - k], x, z, (t + k) % NT)

    for k in range(1, NT):
        e_copy(k).start()

    fraction = (1.0 - FACTOR_DECAY) / BLK
    rows = pl.ds(pl.multiple_of(t * 64, 64), 64)
    local[5].wait()
    right = dot3((hhi[rows, :], hlo[rows, :]), h2, NTR)
    rn_ref[0] = FACTOR_DECAY * rsv[...] + fraction * right

    for k in range(1, NT):
        e_copy(k).wait_recv()
    prec_square = (jnp.sum(sq[...]) + jnp.sum(sq_own[...])) / (BLK * BLK)
    graft = jnp.sqrt(jnp.full((1, 128), (grad_square + GRAFT_EPSILON) / (prec_square + GRAFT_EPSILON), F32))
    upd[...] = (precond * graft).astype(BF16).reshape(NZ, 16, 128)

    def f_send(k):
        to = (z + k) % NZ
        return rc(upd.at[to], fbuf.at[z], f_s.at[k], f_r.at[z], x, to, t)

    for k in offset_of[:0:-1]:
        f_send(k).start()
    f_local = pltpu.make_async_copy(upd.at[z], fbuf.at[z], loc.at[10])
    f_local.start()

    local[4].wait()
    lanes = pl.ds(pl.multiple_of(y * 128, 128), 128)
    left = dot3((hhi[:, lanes], hlo[:, lanes]), h2, TN)
    lgram[...] = left.reshape(2, 64, BLK)
    ln_ref[0] = FACTOR_DECAY * lsv[...] + fraction * lgram[c]

    def find_z(b):
        def step(k, found):
            return jnp.where(ob_ref[x * NZ + k] == b, k, found)

        zsel[b] = lax.fori_loop(0, NZ, step, 0)

    loop(0, NB, find_z)
    for cb in range(2):
        wanted = t * 4 + (x // 2) * 2 + cb

        def step(k, found):
            return jnp.where(ob_ref[k] == wanted, k // NZ, found)

        xsel[cb] = lax.fori_loop(0, NX * NZ, step, 0)

    def f_wait(k):
        src = (z + k) % NZ
        rc(fbuf.at[src], fbuf.at[src], f_s.at[k], f_r.at[src], x, src, t).wait_recv()

    loop(1, NZ, f_wait)
    f_local.wait()

    def h_fill(k):
        rb, to_t = k // NT, k % NT
        for cb in range(2):
            sb2[k, cb] = fbuf[zsel[to_t * 4 + rb * 2 + cb]]

    def h_is_self(k):
        return jnp.logical_and(c + 2 * (k // NT) == x, k % NT == t)

    def h_send(k):
        return rc(sb2.at[k], gr.at[x, y], h_s.at[k], h_r.at[x, y], c + 2 * (k // NT), z, k % NT)

    def h_start(k):
        pl.when(h_is_self(k))(lambda: pltpu.make_async_copy(sb2.at[k], gr.at[x, y], loc.at[8]).start())
        pl.when(jnp.logical_not(h_is_self(k)))(lambda: h_send(k).start())

    loop(0, 16, h_fill)
    loop(0, 16, h_start)

    def h_wait(k):
        from_x, from_y = k // NY, k % NY
        from_t = from_y * 2 + x % 2
        same = jnp.logical_and(from_x == x, from_t == t)
        place = gr.at[from_x, from_y]
        pl.when(same)(lambda: pltpu.make_async_copy(place, place, loc.at[8]).wait())
        pl.when(jnp.logical_not(same))(
            lambda: rc(place, place, h_s.at[0], h_r.at[from_x, from_y], from_x, z, from_t).wait_recv()
        )

    loop(0, 16, h_wait)
    for cb in range(2):
        for row in range(NY):
            dir_ref[:, cb * BLK + row * 128 : cb * BLK + (row + 1) * 128] = gr[xsel[cb], row, cb]

    for copy in x_send + g_send + y_send + d_send + c_send + cd_send + [rr_send]:
        copy.wait_send()
    pl.when(jnp.logical_not(l_self))(lambda: l_send(0).wait_send())
    for j in range(1, NY):
        l_send(j).wait_send()

    for q in chunks:
        for way in ways:
            for m in (7, 5, 3, 1):
                one(q, way, m).wait_send()
            for m in (8, 6, 4, 2)[way > 0 :]:
                two(q, way, m).wait_send()
    pl.when(jnp.logical_not(a_self))(lambda: a_send(0).wait_send())
    loop(1, 16, lambda k: a_send(k).wait_send())
    for k in range(1, NZ):
        b_copy(k).wait_send()
    for k in range(1, NT):
        e_copy(k).wait_send()
    loop(1, NZ, lambda k: f_send(k).wait_send())
    loop(0, 16, lambda k: pl.when(jnp.logical_not(h_is_self(k)))(lambda: h_send(k).wait_send()))


def on_device(inputs, out_grad, left_stat, right_stat, left_root, right_root, owner_blocks):
    anywhere = pl.BlockSpec(memory_space=pltpu.HBM)
    in_vmem = pl.BlockSpec(memory_space=pltpu.VMEM)
    dma = pltpu.SemaphoreType.DMA
    return pl.pallas_call(
        kernel,
        out_shape=(
            jax.ShapeDtypeStruct((1, 64, BLK), F32),
            jax.ShapeDtypeStruct((1, 64, BLK), F32),
            jax.ShapeDtypeStruct((16, 1024), BF16),
        ),
        in_specs=[anywhere] * 6 + [pl.BlockSpec(memory_space=pltpu.SMEM)],
        out_specs=(in_vmem, in_vmem, in_vmem),
        scratch_shapes=[
            pltpu.VMEM((NY, 2, 32, 1024), BF16),
            pltpu.VMEM((NY, 2, 32, 1024), BF16),
            pltpu.VMEM((NY, 2, 32, 1024), BF16),
            pltpu.VMEM((NY, 2, 32, 1024), BF16),
            pltpu.VMEM((2, 256, 128), BF16),
            pltpu.VMEM((2, 256, 128), BF16),
            pltpu.VMEM((2, 256, 128), BF16),
            pltpu.VMEM((2, 256, 128), BF16),
            pltpu.VMEM((2, 2, NZ, 8, BLK), F32),
            pltpu.VMEM((2, 2, 2, 4, 8, BLK), F32),
            pltpu.VMEM((2, 2, 2, 4, 8, BLK), F32),
            pltpu.VMEM((2, 2, 2, 3, 8, BLK), F32),
            pltpu.VMEM((NY, 2, 2, 8, 128), F32),
            pltpu.VMEM((NT, 2, 2, 2, 8, 128), F32),
            pltpu.VMEM((NZ, 2, 8, 128), F32),
            pltpu.VMEM((2, NY, NZ, 2, 8, 128), F32),
            pltpu.VMEM((4, 64, BLK), F32),
            pltpu.VMEM((2, 64, BLK), F32),
            pltpu.VMEM((BLK, BLK), BF16),
            pltpu.VMEM((BLK, BLK), BF16),
            pltpu.VMEM((64, BLK), F32),
            pltpu.VMEM((64, BLK), F32),
            pltpu.VMEM((2, 64, BLK), F32),
            pltpu.VMEM((NT - 1, 8, 128), F32),
            pltpu.VMEM((8, 128), F32),
            pltpu.VMEM((NZ, 16, 128), BF16),
            pltpu.VMEM((NZ, 16, 128), BF16),
            pltpu.VMEM((16, 2, 16, 128), BF16),
            pltpu.VMEM((NX, NY, 2, 16, 128), BF16),
            pltpu.SMEM((NB,), jnp.int32),
            pltpu.SMEM((2,), jnp.int32),
            dma((11,)),
            dma((4, 4)), dma((4, 4)),
            dma((4, 4)), dma((4, 4)),
            dma((4, 4)), dma((4, 4)),
            dma((2, 4)), dma((2, 4)),
            dma((4,)), dma((4,)),
            dma, dma,
            dma((2, 2, 2, 4)), dma((2, 2, 2, 4)), dma((2, 2, 2, 4)), dma((2, 2, 2, 4)),
            dma((16,)), dma((8, 2)),
            dma((16,)), dma((16,)),
            dma((4, 4)), dma((4, 4)), dma((4, 4)), dma((4, 4)),
            dma((8,)), dma((8,)),
            dma((16,)), dma((16,)),
            dma((16,)), dma((4, 4)),
        ],
        compiler_params=pltpu.CompilerParams(
            collective_id=0, has_side_effects=True, vmem_limit_bytes=63 * 1024 * 1024 + 900 * 1024
        ),
        name="shampoo",
    )(
        inputs.reshape(NY, 2, 32, 1024), out_grad, left_stat, right_stat, left_root, right_root,
        owner_blocks.reshape(NX * NZ),
    )


def solution(mesh):
    placed = (
        P("dp", None),
        P("dp", "tensor"),
        P("dp", "tensor", None),
        P("dp", "tensor", None),
        P("dp", "tensor", None),
        P("dp", "tensor", None),
        P(),
    )
    return jax.shard_map(
        on_device,
        mesh=mesh,
        in_specs=placed,
        out_specs=(P("dp", "tensor", None), P("dp", "tensor", None), P("dp", "tensor")),
        check_vma=False,
    )
```

```python
import functools

import jax
import jax.numpy as jnp
from jax import lax
from jax.experimental import pallas as pl
from jax.experimental.pallas import tpu as pltpu
from jax.sharding import PartitionSpec as P

BLK = 512
NX = 4
NY = 4
NZ = 16
NT = 8
NB = 32
FACTOR_DECAY = 0.9
GRAFT_EPSILON = 1e-06
MESH = pl.DeviceIdType.MESH
F32 = jnp.float32
BF16 = jnp.bfloat16

NN = (((1,), (0,)), ((), ()))
NTR = (((1,), (1,)), ((), ()))
TN = (((0,), (0,)), ((), ()))


def dot(a, b, dims):
    return lax.dot_general(a, b, dims, preferred_element_type=F32)


def split(a):
    hi = a.astype(BF16)
    return hi, (a - hi.astype(F32)).astype(BF16)


def dot3(a, b, dims):
    return dot(a[0], b[0], dims) + (dot(a[0], b[1], dims) + dot(a[1], b[0], dims))


def loop(low, high, body):
    def step(k, carry):
        body(k)
        return carry

    lax.fori_loop(low, high, step, 0)


def kernel(
    x_ref, g_ref, ls_ref, rs_ref, lr_ref, rr_ref, ob_ref,
    ln_ref, rn_ref, dir_ref,
    xown, xb1, xb2, xb3, gown, gb1, gb2, gb3, part, ring_1, ring_2, ring_a, own, r1, sb, hrel, lh, rrb, hhi, hlo, lsv, rsv, lgram,
    sq, sq_own, upd, fbuf, sb2, gr, zsel, xsel,
    loc, xs, xr, ys, yr, ds_, dr, gs, gr_s, lsd, lrv, rrs, rrr,
    r1s, r1r, r2s, r2r, a_s, a_r, b_s, b_r, c_s, c_r, cd_s, cd_r, e_s, e_r, f_s, f_r, h_s, h_r,
):
    d = lax.axis_index("dp")
    t = lax.axis_index("tensor")
    x = d // NZ
    z = d % NZ
    y = t // 2
    c = t % 2
    sib = y * 2 + (1 - c)

    def rc(src, dst, ssem, rsem, dx, dz, dt):
        return pltpu.make_async_remote_copy(
            src_ref=src, dst_ref=dst, send_sem=ssem, recv_sem=rsem,
            device_id=(dx * NZ + dz, dt), device_id_type=MESH,
        )

    local = [
        pltpu.make_async_copy(x_ref, xown, loc.at[0]),
        pltpu.make_async_copy(g_ref.at[:, pl.ds(pl.multiple_of(x * 128, 128), 128)], gown.at[0], loc.at[1]),
        pltpu.make_async_copy(g_ref.at[:, pl.ds(pl.multiple_of(512 + x * 128, 128), 128)], gown.at[1], loc.at[2]),
        pltpu.make_async_copy(rr_ref.at[0], rrb.at[c], loc.at[3]),
        pltpu.make_async_copy(ls_ref.at[0], lsv, loc.at[4]),
        pltpu.make_async_copy(rs_ref.at[0], rsv, loc.at[5]),
    ]
    for copy in local:
        copy.start()

    barrier = pltpu.get_barrier_semaphore()
    met = [((x + i) % NX, z, t) for i in (1, 3, 2)] + [(x, z, (t + k) % NT) for k in range(1, NT)]
    met += [(x, (z + k) % NZ, t) for k in (1, NZ - 1, 2, NZ - 2)]
    for to_x, to_z, to_t in met:
        pl.semaphore_signal(barrier, inc=1, device_id=(to_x * NZ + to_z, to_t), device_id_type=MESH)
    pl.semaphore_wait(barrier, len(met))

    order = (1, 3, 2)
    xb = (xown, xb1, xb2, xb3)
    gb = (gown, gb1, gb2, gb3)

    def x_copy(i, j):
        src = x_ref.at[(y + j) % NY, c]
        return rc(src, xb[NX - i].at[j, 0], xs.at[i, j], xr.at[NX - i, j], (x + i) % NX, z, t)

    def g_copy(cb, i):
        to = (x + i) % NX
        columns = pl.ds(pl.multiple_of(cb * BLK + to * 128, 128), 128)
        return rc(g_ref.at[:, columns], gb[NX - i].at[cb], gs.at[cb, i], gr_s.at[cb, NX - i], to, z, t)

    x_send = [x_copy(i, 0) for i in order] + [x_copy(i, 2) for i in (1, 3)]
    g_send = [g_copy(cb, i) for cb in range(2) for i in order]
    for copy in x_send + g_send:
        copy.start()

    for copy in local[:3]:
        copy.wait()

    def gram(act, grads):
        value = dot(jnp.concatenate([grads[0], grads[1]], axis=1), act, TN)
        for cb in range(2):
            for rb in range(2):
                yield cb, rb, value[cb * 128 : cb * 128 + 128, rb * BLK : rb * BLK + BLK].reshape(NZ, 8, BLK)

    for cb, rb, value in gram(xown[...].reshape(256, 1024), gown):
        part[cb, rb] = value

    def y_copy(i, j):
        to = ((y + j) % NY) * 2 + c
        return rc(xb[i].at[0, 0], xb[i].at[NY - j, 0], ys.at[i, j], yr.at[i, NY - j], x, z, to)

    def core_copy(i, j):
        return rc(xb[i].at[j, 0], xb[i].at[j, 1], ds_.at[i, j], dr.at[i, j], x, z, sib)

    y_send, d_send = [], []
    for i in order:
        x_copy(NX - i, 0).wait_recv()
        for j in (1, 3, 2) if i == 2 else (1, 3):
            y_send.append(y_copy(i, j))
            y_send[-1].start()
        d_send.append(core_copy(i, 0))
        d_send[-1].start()

    for i in order:
        for j in (2, 1, 3):
            if j == 2 and i != 2:
                x_copy(NX - i, 2).wait_recv()
            else:
                y_copy(i, NY - j).wait_recv()
            d_send.append(core_copy(i, j))
            d_send[-1].start()
    for i in order:
        for j in range(NY):
            core_copy(i, j).wait_recv()
        for cb in range(2):
            g_copy(cb, NX - i).wait_recv()
        act = jnp.concatenate(
            [xb[i][(row + NY - y) % NY, (core + c) % 2] for row in range(NY) for core in range(2)], axis=0
        )
        for cb, rb, value in gram(act, gb[i]):
            part[cb, rb] += value

    chunks = [(cb, rb) for cb in range(2) for rb in range(2)]
    ways = (-1, 1)

    def ring_to(way, far):
        return (z + NZ + way * far) % NZ

    def one(q, way, m, src=None):
        w = (way + 1) // 2
        src = part.at[*q, 0] if src is None else src
        k = m // 2
        return rc(src, ring_1.at[w, *q, k], r1s.at[w, *q, k], r1r.at[w, *q, k], x, ring_to(way, 1), t)

    def two(q, way, m, src=None):
        w = (way + 1) // 2
        src = part.at[*q, 0] if src is None else src
        k = m // 2 - 1
        return rc(src, ring_2.at[w, *q, k], r2s.at[w, *q, k], r2r.at[w, *q, k], x, ring_to(way, 2), t)

    def ring_one(m):
        for q in chunks:
            for way in ways:
                one(q, way, m, part.at[*q, ring_to(way, m)]).start()

    def gathered(q, way, m):
        w = (way + 1) // 2
        one(q, way, m + 1).wait_recv()
        total = ring_1[w, *q, m // 2]
        if m < (8 if way < 0 else 6) - 1:
            two(q, way, m + 2).wait_recv()
            total = total + ring_2[w, *q, m // 2]
        return total

    for q in chunks:
        two(q, -1, 8, part.at[*q, ring_to(-1, 8)]).start()
        for way in (1, -1):
            one(q, way, 7, part.at[*q, ring_to(way, 7)]).start()
    ring_one(5)
    rr_send = rc(rr_ref.at[0], rrb.at[c], rrs, rrr, x, z, sib)
    rr_send.start()
    l_core = y // 2
    l_self = l_core == c
    l_local = pltpu.make_async_copy(lr_ref.at[0], lh.at[t % 4], loc.at[6])

    def l_send(j):
        return rc(lr_ref.at[0], lh.at[t % 4], lsd.at[j], lrv.at[t % 4], x, z, ((y + j) % NY) * 2 + l_core)

    pl.when(l_self)(lambda: l_local.start())
    pl.when(jnp.logical_not(l_self))(lambda: l_send(0).start())
    for j in range(1, NY):
        l_send(j).start()

    for m in (6, 4, 2):
        for q in chunks:
            for way in ways:
                w = (way + 1) // 2
                ring_a[w, *q, m // 2 - 1] = part[*q, ring_to(way, m)] + gathered(q, way, m)
                two(q, way, m, ring_a.at[w, *q, m // 2 - 1]).start()
        if m > 2:
            ring_one(m - 3)
    for q in chunks:
        total = part[*q, z] + (gathered(q, -1, 0) + gathered(q, 1, 0))
        for row in range(NY):
            own[row, q[1], q[0]] = total[:, row * 128 : row * 128 + 128]

    a_core = x // 2

    def a_copy(k):
        to_x, to_y = (x + k // NY) % NX, (y + k % NY) % NY
        return own.at[to_y], to_x, to_y * 2 + a_core

    def a_send(k):
        src, to_x, to_t = a_copy(k)
        return rc(src, r1.at[t, x % 2], a_s.at[k], a_r.at[t, x % 2], to_x, z, to_t)

    a_local = pltpu.make_async_copy(a_copy(0)[0], r1.at[t, x % 2], loc.at[7])
    a_self = a_core == c
    pl.when(a_self)(lambda: a_local.start())
    pl.when(jnp.logical_not(a_self))(lambda: a_send(0).start())
    for k in sorted(range(1, 16), key=lambda k: -min(k // 4, 4 - k // 4) - min(k % 4, 4 - k % 4)):
        a_send(k).start()
    pl.when(a_self)(lambda: a_local.wait())

    def a_wait(k):
        from_t, half = k // 2, k % 2
        from_x = c * 2 + half

        @pl.when(jnp.logical_or(from_t != t, from_x != x))
        def _():
            piece = r1.at[from_t, half]
            rc(piece, piece, a_s.at[0], a_r.at[from_t, half], from_x, z, from_t).wait_recv()

    loop(0, 16, a_wait)

    def slot_of(o):
        return max(2 * o - 1, 0) if o <= 8 else 2 * NZ - 2 * o

    offset_of = sorted(range(NZ), key=slot_of)

    def b_fill(k):
        block = ob_ref[x * NZ + (z + k) % NZ]
        safe = jnp.minimum(block, NB - 1)
        for half in range(2):
            value = r1[safe // 4, half, (safe // 2) % 2, safe % 2]
            sb[k, half] = jnp.where(block < NB, value, jnp.zeros_like(value))

    def b_copy(k):
        to = (z + k) % NZ
        return rc(sb.at[k], hrel.at[0, 0, slot_of(NZ - k)], b_s.at[k], b_r.at[NZ - k], x, to, t)

    b_local = pltpu.make_async_copy(sb.at[0], hrel.at[0, 0, 0], loc.at[9])
    for o in offset_of:
        b_fill(o)
        if o == 0:
            b_local.start()
        else:
            b_copy(o).start()

    def c_copy(g, j):
        src, dst = hrel.at[0, 0, pl.ds(4 * g, 4)], hrel.at[0, NY - j, pl.ds(4 * g, 4)]
        return rc(src, dst, c_s.at[g, j], c_r.at[g, NY - j], x, z, ((y + j) % NY) * 2 + c)

    def cd_copy(g, j):
        src, dst = hrel.at[0, j, pl.ds(4 * g, 4)], hrel.at[1, j, pl.ds(4 * g, 4)]
        return rc(src, dst, cd_s.at[g, j], cd_r.at[g, j], x, z, sib)

    c_send, cd_send = [], []

    def pass_on(g):
        for j in (1, 3, 2):
            c_copy(g, NY - j).wait_recv()
            cd_copy(g, j).start()
            cd_send.append(cd_copy(g, j))

    for g in range(4):
        for o in offset_of[4 * g : 4 * g + 4]:
            if o == 0:
                b_local.wait()
            else:
                b_copy(NZ - o).wait_recv()
        for j in (1, 3, 2):
            c_copy(g, j).start()
            c_send.append(c_copy(g, j))
        cd_copy(g, 0).start()
        cd_send.append(cd_copy(g, 0))
        if g > 0:
            pass_on(g - 1)
    pass_on(3)
    for copy in cd_send:
        copy.wait_recv()

    local[3].wait()
    rc(rrb.at[1 - c], rrb.at[1 - c], rrs, rrr, x, z, sib).wait_recv()
    pl.when(l_self)(lambda: l_local.wait())

    def l_wait(k):
        from_t = c * 4 + k

        @pl.when(from_t != t)
        def _():
            rc(lh.at[k], lh.at[k], lsd.at[0], lrv.at[k], x, z, from_t).wait_recv()

    loop(0, 4, l_wait)
    def place(row):
        o = (row + NZ - z) % NZ
        return jnp.where(o <= 8, jnp.maximum(2 * o - 1, 0), 2 * NZ - 2 * o)

    def tile(col_x, row_z, row):
        return hrel[(col_x // 2 + c) % 2, (row + NY - y) % NY, place(row_z), col_x % 2]

    h = jnp.concatenate(
        [
            jnp.concatenate([tile(col_x, row_z, row) for row in range(NY)], axis=1)
            for col_x in range(NX)
            for row_z in range(NZ)
        ],
        axis=0,
    )
    hi, lo = split(h)
    hhi[...] = hi
    hlo[...] = lo
    grad_square = jnp.sum(h * h) / (BLK * BLK)
    h2 = (hi, lo)
    turned = dot3(split(rrb[...].reshape(128, BLK)), h2, NN)
    precond = dot3(split(lh[...].reshape(256, BLK)), split(turned), NTR)
    sq_own[...] = jnp.sum((precond * precond).reshape(32, 8, 128), axis=0)

    def e_copy(k):
        return rc(sq_own, sq.at[NT - 1 - k], e_s.at[k], e_r.at[NT - k], x, z, (t + k) % NT)

    for k in range(1, NT):
        e_copy(k).start()

    fraction = (1.0 - FACTOR_DECAY) / BLK
    rows = pl.ds(pl.multiple_of(t * 64, 64), 64)
    local[5].wait()
    right = dot3((hhi[rows, :], hlo[rows, :]), h2, NTR)
    rn_ref[0] = FACTOR_DECAY * rsv[...] + fraction * right

    for k in range(1, NT):
        e_copy(k).wait_recv()
    prec_square = (jnp.sum(sq[...]) + jnp.sum(sq_own[...])) / (BLK * BLK)
    graft = jnp.sqrt(jnp.full((1, 128), (grad_square + GRAFT_EPSILON) / (prec_square + GRAFT_EPSILON), F32))
    upd[...] = (precond * graft).astype(BF16).reshape(NZ, 16, 128)

    def f_send(k):
        to = (z + k) % NZ
        return rc(upd.at[to], fbuf.at[z], f_s.at[k], f_r.at[z], x, to, t)

    for k in offset_of[:0:-1]:
        f_send(k).start()
    f_local = pltpu.make_async_copy(upd.at[z], fbuf.at[z], loc.at[10])
    f_local.start()

    local[4].wait()
    lanes = pl.ds(pl.multiple_of(y * 128, 128), 128)
    left = dot3((hhi[:, lanes], hlo[:, lanes]), h2, TN)
    lgram[...] = left.reshape(2, 64, BLK)
    ln_ref[0] = FACTOR_DECAY * lsv[...] + fraction * lgram[c]

    held = [ob_ref[x * NZ + k] for k in range(NZ)]

    def find_z(b):
        found = 0
        for k in range(NZ):
            found = jnp.where(held[k] == b, k, found)
        zsel[b] = found

    loop(0, NB, find_z)
    wanted = t * 4 + (x // 2) * 2

    def find_x(k, found):
        block = ob_ref[k]
        return tuple(jnp.where(block == wanted + cb, k // NZ, found[cb]) for cb in range(2))

    xsel[0], xsel[1] = lax.fori_loop(0, NX * NZ, find_x, (0, 0))

    def f_wait(k):
        src = (z + k) % NZ
        rc(fbuf.at[src], fbuf.at[src], f_s.at[k], f_r.at[src], x, src, t).wait_recv()

    loop(1, NZ, f_wait)
    f_local.wait()

    def h_fill(k):
        rb, to_t = k // NT, k % NT
        for cb in range(2):
            sb2[k, cb] = fbuf[zsel[to_t * 4 + rb * 2 + cb]]

    def h_is_self(k):
        return jnp.logical_and(c + 2 * (k // NT) == x, k % NT == t)

    def h_send(k):
        return rc(sb2.at[k], gr.at[x, y], h_s.at[k], h_r.at[x, y], c + 2 * (k // NT), z, k % NT)

    def h_start(k):
        pl.when(h_is_self(k))(lambda: pltpu.make_async_copy(sb2.at[k], gr.at[x, y], loc.at[8]).start())
        pl.when(jnp.logical_not(h_is_self(k)))(lambda: h_send(k).start())

    loop(0, 16, h_fill)
    loop(0, 16, h_start)

    def h_wait(k):
        from_x, from_y = k // NY, k % NY
        from_t = from_y * 2 + x % 2
        same = jnp.logical_and(from_x == x, from_t == t)
        place = gr.at[from_x, from_y]
        pl.when(same)(lambda: pltpu.make_async_copy(place, place, loc.at[8]).wait())
        pl.when(jnp.logical_not(same))(
            lambda: rc(place, place, h_s.at[0], h_r.at[from_x, from_y], from_x, z, from_t).wait_recv()
        )

    loop(0, 16, h_wait)
    for cb in range(2):
        for row in range(NY):
            dir_ref[:, cb * BLK + row * 128 : cb * BLK + (row + 1) * 128] = gr[xsel[cb], row, cb]

    for copy in x_send + g_send + y_send + d_send + c_send + cd_send + [rr_send]:
        copy.wait_send()
    pl.when(jnp.logical_not(l_self))(lambda: l_send(0).wait_send())
    for j in range(1, NY):
        l_send(j).wait_send()

    for q in chunks:
        for way in ways:
            for m in (7, 5, 3, 1):
                one(q, way, m).wait_send()
            for m in (8, 6, 4, 2)[way > 0 :]:
                two(q, way, m).wait_send()
    pl.when(jnp.logical_not(a_self))(lambda: a_send(0).wait_send())
    loop(1, 16, lambda k: a_send(k).wait_send())
    for k in range(1, NZ):
        b_copy(k).wait_send()
    for k in range(1, NT):
        e_copy(k).wait_send()
    loop(1, NZ, lambda k: f_send(k).wait_send())
    loop(0, 16, lambda k: pl.when(jnp.logical_not(h_is_self(k)))(lambda: h_send(k).wait_send()))


def on_device(inputs, out_grad, left_stat, right_stat, left_root, right_root, owner_blocks):
    anywhere = pl.BlockSpec(memory_space=pltpu.HBM)
    in_vmem = pl.BlockSpec(memory_space=pltpu.VMEM)
    dma = pltpu.SemaphoreType.DMA
    return pl.pallas_call(
        kernel,
        out_shape=(
            jax.ShapeDtypeStruct((1, 64, BLK), F32),
            jax.ShapeDtypeStruct((1, 64, BLK), F32),
            jax.ShapeDtypeStruct((16, 1024), BF16),
        ),
        in_specs=[anywhere] * 6 + [pl.BlockSpec(memory_space=pltpu.SMEM)],
        out_specs=(in_vmem, in_vmem, in_vmem),
        scratch_shapes=[
            pltpu.VMEM((NY, 2, 32, 1024), BF16),
            pltpu.VMEM((NY, 2, 32, 1024), BF16),
            pltpu.VMEM((NY, 2, 32, 1024), BF16),
            pltpu.VMEM((NY, 2, 32, 1024), BF16),
            pltpu.VMEM((2, 256, 128), BF16),
            pltpu.VMEM((2, 256, 128), BF16),
            pltpu.VMEM((2, 256, 128), BF16),
            pltpu.VMEM((2, 256, 128), BF16),
            pltpu.VMEM((2, 2, NZ, 8, BLK), F32),
            pltpu.VMEM((2, 2, 2, 4, 8, BLK), F32),
            pltpu.VMEM((2, 2, 2, 4, 8, BLK), F32),
            pltpu.VMEM((2, 2, 2, 3, 8, BLK), F32),
            pltpu.VMEM((NY, 2, 2, 8, 128), F32),
            pltpu.VMEM((NT, 2, 2, 2, 8, 128), F32),
            pltpu.VMEM((NZ, 2, 8, 128), F32),
            pltpu.VMEM((2, NY, NZ, 2, 8, 128), F32),
            pltpu.VMEM((4, 64, BLK), F32),
            pltpu.VMEM((2, 64, BLK), F32),
            pltpu.VMEM((BLK, BLK), BF16),
            pltpu.VMEM((BLK, BLK), BF16),
            pltpu.VMEM((64, BLK), F32),
            pltpu.VMEM((64, BLK), F32),
            pltpu.VMEM((2, 64, BLK), F32),
            pltpu.VMEM((NT - 1, 8, 128), F32),
            pltpu.VMEM((8, 128), F32),
            pltpu.VMEM((NZ, 16, 128), BF16),
            pltpu.VMEM((NZ, 16, 128), BF16),
            pltpu.VMEM((16, 2, 16, 128), BF16),
            pltpu.VMEM((NX, NY, 2, 16, 128), BF16),
            pltpu.SMEM((NB,), jnp.int32),
            pltpu.SMEM((2,), jnp.int32),
            dma((11,)),
            dma((4, 4)), dma((4, 4)),
            dma((4, 4)), dma((4, 4)),
            dma((4, 4)), dma((4, 4)),
            dma((2, 4)), dma((2, 4)),
            dma((4,)), dma((4,)),
            dma, dma,
            dma((2, 2, 2, 4)), dma((2, 2, 2, 4)), dma((2, 2, 2, 4)), dma((2, 2, 2, 4)),
            dma((16,)), dma((8, 2)),
            dma((16,)), dma((16,)),
            dma((4, 4)), dma((4, 4)), dma((4, 4)), dma((4, 4)),
            dma((8,)), dma((8,)),
            dma((16,)), dma((16,)),
            dma((16,)), dma((4, 4)),
        ],
        compiler_params=pltpu.CompilerParams(
            collective_id=0, has_side_effects=True, vmem_limit_bytes=63 * 1024 * 1024 + 900 * 1024
        ),
        name="shampoo",
    )(
        inputs.reshape(NY, 2, 32, 1024), out_grad, left_stat, right_stat, left_root, right_root,
        owner_blocks.reshape(NX * NZ),
    )


def solution(mesh):
    placed = (
        P("dp", None),
        P("dp", "tensor"),
        P("dp", "tensor", None),
        P("dp", "tensor", None),
        P("dp", "tensor", None),
        P("dp", "tensor", None),
        P(),
    )
    return jax.shard_map(
        on_device,
        mesh=mesh,
        in_specs=placed,
        out_specs=(P("dp", "tensor", None), P("dp", "tensor", None), P("dp", "tensor")),
        check_vma=False,
    )
```

```python
import functools

import jax
import jax.numpy as jnp
from jax import lax
from jax.experimental import pallas as pl
from jax.experimental.pallas import tpu as pltpu
from jax.sharding import PartitionSpec as P

BLK = 512
NX = 4
NY = 4
NZ = 16
NT = 8
NB = 32
FACTOR_DECAY = 0.9
GRAFT_EPSILON = 1e-06
MESH = pl.DeviceIdType.MESH
F32 = jnp.float32
BF16 = jnp.bfloat16

NN = (((1,), (0,)), ((), ()))
NTR = (((1,), (1,)), ((), ()))
TN = (((0,), (0,)), ((), ()))


def dot(a, b, dims):
    return lax.dot_general(a, b, dims, preferred_element_type=F32)


def split(a):
    hi = a.astype(BF16)
    return hi, (a - hi.astype(F32)).astype(BF16)


def dot3(a, b, dims):
    return dot(a[0], b[0], dims) + (dot(a[0], b[1], dims) + dot(a[1], b[0], dims))


def loop(low, high, body):
    def step(k, carry):
        body(k)
        return carry

    lax.fori_loop(low, high, step, 0)


def kernel(
    x_ref, g_ref, ls_ref, rs_ref, lr_ref, rr_ref, ob_ref,
    ln_ref, rn_ref, dir_ref,
    xown, xb1, xb2, xb3, gown, gb1, gb2, gb3, part, ring_1, ring_2, ring_a, own, r1, sb, hrel, lh, rrb, hhi, hlo, lsv, rsv, lgram,
    sq, sq_own, upd, fbuf, sb2, gr, zsel, xsel,
    loc, xs, xr, ys, yr, ds_, dr, gs, gr_s, lsd, lrv, rrs, rrr,
    r1s, r1r, r2s, r2r, a_s, a_r, b_s, b_r, c_s, c_r, cd_s, cd_r, e_s, e_r, f_s, f_r, h_s, h_r,
):
    d = lax.axis_index("dp")
    t = lax.axis_index("tensor")
    x = d // NZ
    z = d % NZ
    y = t // 2
    c = t % 2
    sib = y * 2 + (1 - c)

    def rc(src, dst, ssem, rsem, dx, dz, dt):
        return pltpu.make_async_remote_copy(
            src_ref=src, dst_ref=dst, send_sem=ssem, recv_sem=rsem,
            device_id=(dx * NZ + dz, dt), device_id_type=MESH,
        )

    local = [
        pltpu.make_async_copy(x_ref, xown, loc.at[0]),
        pltpu.make_async_copy(g_ref.at[:, pl.ds(pl.multiple_of(x * 128, 128), 128)], gown.at[0], loc.at[1]),
        pltpu.make_async_copy(g_ref.at[:, pl.ds(pl.multiple_of(512 + x * 128, 128), 128)], gown.at[1], loc.at[2]),
        pltpu.make_async_copy(rr_ref.at[0], rrb.at[c], loc.at[3]),
        pltpu.make_async_copy(ls_ref.at[0], lsv, loc.at[4]),
        pltpu.make_async_copy(rs_ref.at[0], rsv, loc.at[5]),
    ]
    for copy in local:
        copy.start()

    barrier = pltpu.get_barrier_semaphore()
    met = [((x + i) % NX, z, t) for i in (1, 3, 2)] + [(x, z, (t + k) % NT) for k in range(1, NT)]
    met += [(x, (z + k) % NZ, t) for k in (1, NZ - 1, 2, NZ - 2)]
    for to_x, to_z, to_t in met:
        pl.semaphore_signal(barrier, inc=1, device_id=(to_x * NZ + to_z, to_t), device_id_type=MESH)
    pl.semaphore_wait(barrier, len(met))

    order = (1, 3, 2)
    xb = (xown, xb1, xb2, xb3)
    gb = (gown, gb1, gb2, gb3)

    def x_copy(i, j):
        src = x_ref.at[(y + j) % NY, c]
        return rc(src, xb[NX - i].at[j, 0], xs.at[i, j], xr.at[NX - i, j], (x + i) % NX, z, t)

    def g_copy(cb, i):
        to = (x + i) % NX
        columns = pl.ds(pl.multiple_of(cb * BLK + to * 128, 128), 128)
        return rc(g_ref.at[:, columns], gb[NX - i].at[cb], gs.at[cb, i], gr_s.at[cb, NX - i], to, z, t)

    x_send = [x_copy(i, 0) for i in order] + [x_copy(i, 2) for i in (1, 3)]
    g_send = [g_copy(cb, i) for cb in range(2) for i in order]
    for copy in x_send + g_send:
        copy.start()

    for copy in local[:3]:
        copy.wait()

    def gram(act, grads):
        value = dot(jnp.concatenate([grads[0], grads[1]], axis=1), act, TN)
        for cb in range(2):
            for rb in range(2):
                yield cb, rb, value[cb * 128 : cb * 128 + 128, rb * BLK : rb * BLK + BLK].reshape(NZ, 8, BLK)

    for cb, rb, value in gram(xown[...].reshape(256, 1024), gown):
        part[cb, rb] = value

    def y_copy(i, j):
        to = ((y + j) % NY) * 2 + c
        return rc(xb[i].at[0, 0], xb[i].at[NY - j, 0], ys.at[i, j], yr.at[i, NY - j], x, z, to)

    def core_copy(i, j):
        return rc(xb[i].at[j, 0], xb[i].at[j, 1], ds_.at[i, j], dr.at[i, j], x, z, sib)

    y_send, d_send = [], []
    for i in order:
        x_copy(NX - i, 0).wait_recv()
        for j in (1, 3, 2) if i == 2 else (1, 3):
            y_send.append(y_copy(i, j))
            y_send[-1].start()
        d_send.append(core_copy(i, 0))
        d_send[-1].start()

    for i in order:
        for j in (2, 1, 3):
            if j == 2 and i != 2:
                x_copy(NX - i, 2).wait_recv()
            else:
                y_copy(i, NY - j).wait_recv()
            d_send.append(core_copy(i, j))
            d_send[-1].start()
    for i in order:
        for j in range(NY):
            core_copy(i, j).wait_recv()
        for cb in range(2):
            g_copy(cb, NX - i).wait_recv()
        act = jnp.concatenate(
            [xb[i][(row + NY - y) % NY, (core + c) % 2] for row in range(NY) for core in range(2)], axis=0
        )
        for cb, rb, value in gram(act, gb[i]):
            part[cb, rb] += value

    chunks = [(cb, rb) for cb in range(2) for rb in range(2)]
    ways = (-1, 1)

    def ring_to(way, far):
        return (z + NZ + way * far) % NZ

    def one(q, way, m, src=None):
        w = (way + 1) // 2
        src = part.at[*q, 0] if src is None else src
        k = m // 2
        return rc(src, ring_1.at[w, *q, k], r1s.at[w, *q, k], r1r.at[w, *q, k], x, ring_to(way, 1), t)

    def two(q, way, m, src=None):
        w = (way + 1) // 2
        src = part.at[*q, 0] if src is None else src
        k = m // 2 - 1
        return rc(src, ring_2.at[w, *q, k], r2s.at[w, *q, k], r2r.at[w, *q, k], x, ring_to(way, 2), t)

    def ring_one(m):
        for q in chunks:
            for way in ways:
                one(q, way, m, part.at[*q, ring_to(way, m)]).start()

    def gathered(q, way, m):
        w = (way + 1) // 2
        one(q, way, m + 1).wait_recv()
        total = ring_1[w, *q, m // 2]
        if m < (8 if way < 0 else 6) - 1:
            two(q, way, m + 2).wait_recv()
            total = total + ring_2[w, *q, m // 2]
        return total

    for q in chunks:
        two(q, -1, 8, part.at[*q, ring_to(-1, 8)]).start()
        for way in (1, -1):
            one(q, way, 7, part.at[*q, ring_to(way, 7)]).start()
    ring_one(5)
    rr_send = rc(rr_ref.at[0], rrb.at[c], rrs, rrr, x, z, sib)
    rr_send.start()
    l_core = y // 2
    l_self = l_core == c
    l_local = pltpu.make_async_copy(lr_ref.at[0], lh.at[t % 4], loc.at[6])

    def l_send(j):
        return rc(lr_ref.at[0], lh.at[t % 4], lsd.at[j], lrv.at[t % 4], x, z, ((y + j) % NY) * 2 + l_core)

    pl.when(l_self)(lambda: l_local.start())
    pl.when(jnp.logical_not(l_self))(lambda: l_send(0).start())
    for j in range(1, NY):
        l_send(j).start()

    for m in (6, 4, 2):
        for q in chunks:
            for way in ways:
                w = (way + 1) // 2
                ring_a[w, *q, m // 2 - 1] = part[*q, ring_to(way, m)] + gathered(q, way, m)
                two(q, way, m, ring_a.at[w, *q, m // 2 - 1]).start()
        if m > 2:
            ring_one(m - 3)
    for q in chunks:
        total = part[*q, z] + (gathered(q, -1, 0) + gathered(q, 1, 0))
        for row in range(NY):
            own[row, q[1], q[0]] = total[:, row * 128 : row * 128 + 128]

    a_core = x // 2

    def a_copy(k):
        to_x, to_y = (x + k // NY) % NX, (y + k % NY) % NY
        return own.at[to_y], to_x, to_y * 2 + a_core

    def a_send(k):
        src, to_x, to_t = a_copy(k)
        return rc(src, r1.at[t, x % 2], a_s.at[k], a_r.at[t, x % 2], to_x, z, to_t)

    a_local = pltpu.make_async_copy(a_copy(0)[0], r1.at[t, x % 2], loc.at[7])
    a_self = a_core == c
    pl.when(a_self)(lambda: a_local.start())
    pl.when(jnp.logical_not(a_self))(lambda: a_send(0).start())
    for k in sorted(range(1, 16), key=lambda k: -min(k // 4, 4 - k // 4) - min(k % 4, 4 - k % 4)):
        a_send(k).start()
    for copy in x_send + g_send + y_send + d_send:
        copy.wait_send()
    pl.when(a_self)(lambda: a_local.wait())

    def a_wait(k):
        from_t, half = k // 2, k % 2
        from_x = c * 2 + half

        @pl.when(jnp.logical_or(from_t != t, from_x != x))
        def _():
            piece = r1.at[from_t, half]
            rc(piece, piece, a_s.at[0], a_r.at[from_t, half], from_x, z, from_t).wait_recv()

    loop(0, 16, a_wait)

    def slot_of(o):
        return max(2 * o - 1, 0) if o <= 8 else 2 * NZ - 2 * o

    offset_of = sorted(range(NZ), key=slot_of)

    def b_fill(k):
        block = ob_ref[x * NZ + (z + k) % NZ]
        safe = jnp.minimum(block, NB - 1)
        for half in range(2):
            value = r1[safe // 4, half, (safe // 2) % 2, safe % 2]
            sb[k, half] = jnp.where(block < NB, value, jnp.zeros_like(value))

    def b_copy(k):
        to = (z + k) % NZ
        return rc(sb.at[k], hrel.at[0, 0, slot_of(NZ - k)], b_s.at[k], b_r.at[NZ - k], x, to, t)

    b_local = pltpu.make_async_copy(sb.at[0], hrel.at[0, 0, 0], loc.at[9])
    for o in offset_of:
        b_fill(o)
        if o == 0:
            b_local.start()
        else:
            b_copy(o).start()

    def c_copy(g, j):
        src, dst = hrel.at[0, 0, pl.ds(4 * g, 4)], hrel.at[0, NY - j, pl.ds(4 * g, 4)]
        return rc(src, dst, c_s.at[g, j], c_r.at[g, NY - j], x, z, ((y + j) % NY) * 2 + c)

    def cd_copy(g, j):
        src, dst = hrel.at[0, j, pl.ds(4 * g, 4)], hrel.at[1, j, pl.ds(4 * g, 4)]
        return rc(src, dst, cd_s.at[g, j], cd_r.at[g, j], x, z, sib)

    c_send, cd_send = [], []

    def pass_on(g):
        for j in (1, 3, 2):
            c_copy(g, NY - j).wait_recv()
            cd_copy(g, j).start()
            cd_send.append(cd_copy(g, j))

    for g in range(4):
        for o in offset_of[4 * g : 4 * g + 4]:
            if o == 0:
                b_local.wait()
            else:
                b_copy(NZ - o).wait_recv()
        for j in (1, 3, 2):
            c_copy(g, j).start()
            c_send.append(c_copy(g, j))
        cd_copy(g, 0).start()
        cd_send.append(cd_copy(g, 0))
        if g > 0:
            pass_on(g - 1)
    pass_on(3)
    for copy in cd_send:
        copy.wait_recv()

    local[3].wait()
    rc(rrb.at[1 - c], rrb.at[1 - c], rrs, rrr, x, z, sib).wait_recv()
    pl.when(l_self)(lambda: l_local.wait())

    def l_wait(k):
        from_t = c * 4 + k

        @pl.when(from_t != t)
        def _():
            rc(lh.at[k], lh.at[k], lsd.at[0], lrv.at[k], x, z, from_t).wait_recv()

    loop(0, 4, l_wait)
    def place(row):
        o = (row + NZ - z) % NZ
        return jnp.where(o <= 8, jnp.maximum(2 * o - 1, 0), 2 * NZ - 2 * o)

    def tile(col_x, row_z, row):
        return hrel[(col_x // 2 + c) % 2, (row + NY - y) % NY, place(row_z), col_x % 2]

    h = jnp.concatenate(
        [
            jnp.concatenate([tile(col_x, row_z, row) for row in range(NY)], axis=1)
            for col_x in range(NX)
            for row_z in range(NZ)
        ],
        axis=0,
    )
    hi, lo = split(h)
    hhi[...] = hi
    hlo[...] = lo
    grad_square = jnp.sum(h * h) / (BLK * BLK)
    h2 = (hi, lo)
    turned = dot3(split(rrb[...].reshape(128, BLK)), h2, NN)
    precond = dot3(split(lh[...].reshape(256, BLK)), split(turned), NTR)
    sq_own[...] = jnp.sum((precond * precond).reshape(32, 8, 128), axis=0)

    def e_copy(k):
        return rc(sq_own, sq.at[NT - 1 - k], e_s.at[k], e_r.at[NT - k], x, z, (t + k) % NT)

    for k in range(1, NT):
        e_copy(k).start()

    fraction = (1.0 - FACTOR_DECAY) / BLK
    rows = pl.ds(pl.multiple_of(t * 64, 64), 64)
    local[5].wait()
    right = dot3((hhi[rows, :], hlo[rows, :]), h2, NTR)
    rsv[...] = FACTOR_DECAY * rsv[...] + fraction * right
    r_out = pltpu.make_async_copy(rsv, rn_ref.at[0], loc.at[11])
    r_out.start()

    for k in range(1, NT):
        e_copy(k).wait_recv()
    prec_square = (jnp.sum(sq[...]) + jnp.sum(sq_own[...])) / (BLK * BLK)
    graft = jnp.sqrt(jnp.full((1, 128), (grad_square + GRAFT_EPSILON) / (prec_square + GRAFT_EPSILON), F32))
    upd[...] = (precond * graft).astype(BF16).reshape(NZ, 16, 128)

    def f_send(k):
        to = (z + k) % NZ
        return rc(upd.at[to], fbuf.at[z], f_s.at[k], f_r.at[z], x, to, t)

    for k in offset_of[:0:-1]:
        f_send(k).start()
    f_local = pltpu.make_async_copy(upd.at[z], fbuf.at[z], loc.at[10])
    f_local.start()

    local[4].wait()
    lanes = pl.ds(pl.multiple_of(y * 128, 128), 128)
    left = dot3((hhi[:, lanes], hlo[:, lanes]), h2, TN)
    lgram[...] = left.reshape(2, 64, BLK)
    lsv[...] = FACTOR_DECAY * lsv[...] + fraction * lgram[c]
    l_out = pltpu.make_async_copy(lsv, ln_ref.at[0], loc.at[12])
    l_out.start()

    held = [ob_ref[x * NZ + k] for k in range(NZ)]

    def find_z(b):
        found = 0
        for k in range(NZ):
            found = jnp.where(held[k] == b, k, found)
        zsel[b] = found

    loop(0, NB, find_z)
    wanted = t * 4 + (x // 2) * 2

    def find_x(k, found):
        block = ob_ref[k]
        return tuple(jnp.where(block == wanted + cb, k // NZ, found[cb]) for cb in range(2))

    xsel[0], xsel[1] = lax.fori_loop(0, NX * NZ, find_x, (0, 0))

    for copy in c_send + cd_send + [rr_send]:
        copy.wait_send()
    pl.when(jnp.logical_not(l_self))(lambda: l_send(0).wait_send())
    for j in range(1, NY):
        l_send(j).wait_send()

    for q in chunks:
        for way in ways:
            for m in (7, 5, 3, 1):
                one(q, way, m).wait_send()
            for m in (8, 6, 4, 2)[way > 0 :]:
                two(q, way, m).wait_send()
    pl.when(jnp.logical_not(a_self))(lambda: a_send(0).wait_send())
    loop(1, 16, lambda k: a_send(k).wait_send())
    for k in range(1, NZ):
        b_copy(k).wait_send()

    def f_wait(k):
        src = (z + k) % NZ
        rc(fbuf.at[src], fbuf.at[src], f_s.at[k], f_r.at[src], x, src, t).wait_recv()

    loop(1, NZ, f_wait)
    f_local.wait()

    def h_fill(k):
        rb, to_t = k // NT, k % NT
        for cb in range(2):
            sb2[k, cb] = fbuf[zsel[to_t * 4 + rb * 2 + cb]]

    def h_is_self(k):
        return jnp.logical_and(c + 2 * (k // NT) == x, k % NT == t)

    def h_send(k):
        return rc(sb2.at[k], gr.at[x, y], h_s.at[k], h_r.at[x, y], c + 2 * (k // NT), z, k % NT)

    def h_start(k):
        pl.when(h_is_self(k))(lambda: pltpu.make_async_copy(sb2.at[k], gr.at[x, y], loc.at[8]).start())
        pl.when(jnp.logical_not(h_is_self(k)))(lambda: h_send(k).start())

    for k in range(16):
        h_fill(k)
        h_start(k)

    def h_wait(k):
        from_x, from_y = k // NY, k % NY
        from_t = from_y * 2 + x % 2
        same = jnp.logical_and(from_x == x, from_t == t)
        place = gr.at[from_x, from_y]
        pl.when(same)(lambda: pltpu.make_async_copy(place, place, loc.at[8]).wait())
        pl.when(jnp.logical_not(same))(
            lambda: rc(place, place, h_s.at[0], h_r.at[from_x, from_y], from_x, z, from_t).wait_recv()
        )

    loop(0, 16, h_wait)
    for cb in range(2):
        for row in range(NY):
            dir_ref[:, cb * BLK + row * 128 : cb * BLK + (row + 1) * 128] = gr[xsel[cb], row, cb]

    r_out.wait()
    l_out.wait()
    for k in range(1, NT):
        e_copy(k).wait_send()
    loop(1, NZ, lambda k: f_send(k).wait_send())
    loop(0, 16, lambda k: pl.when(jnp.logical_not(h_is_self(k)))(lambda: h_send(k).wait_send()))


def on_device(inputs, out_grad, left_stat, right_stat, left_root, right_root, owner_blocks):
    anywhere = pl.BlockSpec(memory_space=pltpu.HBM)
    in_vmem = pl.BlockSpec(memory_space=pltpu.VMEM)
    dma = pltpu.SemaphoreType.DMA
    return pl.pallas_call(
        kernel,
        out_shape=(
            jax.ShapeDtypeStruct((1, 64, BLK), F32),
            jax.ShapeDtypeStruct((1, 64, BLK), F32),
            jax.ShapeDtypeStruct((16, 1024), BF16),
        ),
        in_specs=[anywhere] * 6 + [pl.BlockSpec(memory_space=pltpu.SMEM)],
        out_specs=(anywhere, anywhere, in_vmem),
        scratch_shapes=[
            pltpu.VMEM((NY, 2, 32, 1024), BF16),
            pltpu.VMEM((NY, 2, 32, 1024), BF16),
            pltpu.VMEM((NY, 2, 32, 1024), BF16),
            pltpu.VMEM((NY, 2, 32, 1024), BF16),
            pltpu.VMEM((2, 256, 128), BF16),
            pltpu.VMEM((2, 256, 128), BF16),
            pltpu.VMEM((2, 256, 128), BF16),
            pltpu.VMEM((2, 256, 128), BF16),
            pltpu.VMEM((2, 2, NZ, 8, BLK), F32),
            pltpu.VMEM((2, 2, 2, 4, 8, BLK), F32),
            pltpu.VMEM((2, 2, 2, 4, 8, BLK), F32),
            pltpu.VMEM((2, 2, 2, 3, 8, BLK), F32),
            pltpu.VMEM((NY, 2, 2, 8, 128), F32),
            pltpu.VMEM((NT, 2, 2, 2, 8, 128), F32),
            pltpu.VMEM((NZ, 2, 8, 128), F32),
            pltpu.VMEM((2, NY, NZ, 2, 8, 128), F32),
            pltpu.VMEM((4, 64, BLK), F32),
            pltpu.VMEM((2, 64, BLK), F32),
            pltpu.VMEM((BLK, BLK), BF16),
            pltpu.VMEM((BLK, BLK), BF16),
            pltpu.VMEM((64, BLK), F32),
            pltpu.VMEM((64, BLK), F32),
            pltpu.VMEM((2, 64, BLK), F32),
            pltpu.VMEM((NT - 1, 8, 128), F32),
            pltpu.VMEM((8, 128), F32),
            pltpu.VMEM((NZ, 16, 128), BF16),
            pltpu.VMEM((NZ, 16, 128), BF16),
            pltpu.VMEM((16, 2, 16, 128), BF16),
            pltpu.VMEM((NX, NY, 2, 16, 128), BF16),
            pltpu.SMEM((NB,), jnp.int32),
            pltpu.SMEM((2,), jnp.int32),
            dma((13,)),
            dma((4, 4)), dma((4, 4)),
            dma((4, 4)), dma((4, 4)),
            dma((4, 4)), dma((4, 4)),
            dma((2, 4)), dma((2, 4)),
            dma((4,)), dma((4,)),
            dma, dma,
            dma((2, 2, 2, 4)), dma((2, 2, 2, 4)), dma((2, 2, 2, 4)), dma((2, 2, 2, 4)),
            dma((16,)), dma((8, 2)),
            dma((16,)), dma((16,)),
            dma((4, 4)), dma((4, 4)), dma((4, 4)), dma((4, 4)),
            dma((8,)), dma((8,)),
            dma((16,)), dma((16,)),
            dma((16,)), dma((4, 4)),
        ],
        compiler_params=pltpu.CompilerParams(
            collective_id=0, has_side_effects=True, vmem_limit_bytes=63 * 1024 * 1024 + 900 * 1024
        ),
        name="shampoo",
    )(
        inputs.reshape(NY, 2, 32, 1024), out_grad, left_stat, right_stat, left_root, right_root,
        owner_blocks.reshape(NX * NZ),
    )


def solution(mesh):
    placed = (
        P("dp", None),
        P("dp", "tensor"),
        P("dp", "tensor", None),
        P("dp", "tensor", None),
        P("dp", "tensor", None),
        P("dp", "tensor", None),
        P(),
    )
    return jax.shard_map(
        on_device,
        mesh=mesh,
        in_specs=placed,
        out_specs=(P("dp", "tensor", None), P("dp", "tensor", None), P("dp", "tensor")),
        check_vma=False,
    )
```
